128 devices in a mesh: tm: 2 (over x_hi), chan: 64 (over y, x_lo, z, core).
Axes of the slice: x: 4 (x_hi: 2, x_lo: 2; x = x_hi * 2 + x_lo), y: 4, z: 4, core: 2. Of those that a mesh axis runs over, the one named last changes fastest.
Arguments:
- strain: bfloat16 [6, 16000, 4096], P('tm', 'chan'), may hold values from -6 to 6
- live_mask: int32 [4096], P('chan'), may hold values 0 or 1
- block_pairs: int32 [2, 64, 2], P(None, 'chan'), may hold values from 0 to 63, as said below
Outputs:
- correlations: bfloat16 [2, 64, 64, 64, 1024], P('tm', 'chan')
The draws below stay inside these ranges and needn't reach their ends.
Inputs may be any that keep to these rules, and one draw needn't show every extreme that they name: `block_pairs`: each row holds two channel-block numbers, the first not above the second; every block number appears in some row.
All inputs are finite; a program needn't handle non-finite values. No bound on the sum of `live_mask` on one device may be relied on, other than what follows from the above.
Results may differ from the reference program's by a relative error of at most 0.01.
Values may be sent and summed in bfloat16 or wider, within the bound.
No kernel may reach another device: no remote copies, remote signals or barrier semaphores. Data moves between devices by JAX's collectives and lax.ppermute only.
A program may use at most 128 MiB of HBM per device.

```python
import math
import jax
import jax.numpy as jnp
from jax import lax

CB = 64
C = 4096
W = 16000
WIN_DEV = 3
NWIN = 6
K0 = 64
F = 256
HALF = 32
LAGS = 1024
PAIRS_HALF = 1
N_TM = 2
N_CHAN = 64


def draw_block_pairs(key, part):
    key = jax.random.fold_in(key, 11)
    first_key, second_key = jax.random.split(key)
    repeats = N_TM * PAIRS_HALF
    first_perm = jax.vmap(lambda single: jax.random.permutation(single, N_CHAN))(jax.random.split(first_key, repeats)).reshape(-1)
    second_perm = jax.vmap(lambda single: jax.random.permutation(single, N_CHAN))(jax.random.split(second_key, repeats)).reshape(-1)
    lower = jnp.minimum(first_perm, second_perm).astype(jnp.int32)
    upper = jnp.maximum(first_perm, second_perm).astype(jnp.int32)
    return jnp.stack([lower, upper], -1).reshape(N_TM, N_CHAN * PAIRS_HALF, 2)


def set_ends(array, own_key, low, largest):
    extent = array.shape
    place = [jax.random.randint(jax.random.fold_in(own_key, axis), (), 0, extent[axis]) for axis in range(len(extent))]
    array = array.at[tuple(place)].set(low)
    longest = extent.index(max(extent))
    place[longest] = (place[longest] + 1) % extent[longest]
    return array.at[tuple(place)].set(largest)


def shard_levels(own_key, extent, shards, low, high):
    gain, own = 1.0, jax.random.fold_in(own_key, 6)
    for axis_at, parts in shards:
        draws = jnp.exp(jax.random.uniform(jax.random.fold_in(own, axis_at), (parts,), jnp.float32, low / len(shards), high / len(shards)))
        gain = gain * jnp.repeat(draws, extent[axis_at] // parts).reshape([-1 if axis == axis_at else 1 for axis in range(len(extent))])
    return gain


def gaussian(rng, shape, scale, bound, shards=(), kind=jnp.bfloat16):
    values = scale * jax.random.normal(rng, shape, jnp.float32)
    if shards:
        values = values * shard_levels(rng, shape, shards, -0.22, 0.18)
    return jnp.clip(values, -bound, bound).astype(kind)


def setup_inputs(seed: int = 0) -> dict:
    arg_keys = jax.random.split(jax.random.key(seed), 4)
    return {
        "strain": gaussian(arg_keys[0], (NWIN, W, C), 1.0, 6.0, ((0, 2), (1, 64))),
        "live_mask": set_ends((jax.random.randint(arg_keys[1], (C,), 0, 8) < 7).astype(jnp.int32), jax.random.fold_in(arg_keys[1], 1), 0, 1),
        "block_pairs": draw_block_pairs(jax.random.fold_in(arg_keys[3], 71), 0),
    }


whiten_eps = 1e-05

def forward_table():
    samples = jnp.arange(W, dtype=jnp.int32)[:, None]
    bins = (K0 - HALF + jnp.arange(F + 2 * HALF, dtype=jnp.int32))[None, :]
    phase_index = samples * bins % W
    angles = 2.0 * math.pi / W * phase_index.astype(jnp.float32)
    window_shape = 0.5 - 0.5 * jnp.cos(2.0 * math.pi / W * jnp.arange(W, dtype=jnp.int32).astype(jnp.float32))[:, None]
    return jnp.concatenate([jnp.cos(angles) * window_shape, -jnp.sin(angles) * window_shape], 1).astype(jnp.bfloat16)

def backward_table():
    freqs = (K0 + jnp.arange(F, dtype=jnp.int32))[:, None]
    lag_steps = (jnp.arange(LAGS, dtype=jnp.int32) - LAGS // 2)[None, :]
    phase_index = freqs * lag_steps % W
    angles = 2.0 * math.pi / W * phase_index.astype(jnp.float32)
    factor = 1.0 / math.sqrt(WIN_DEV * F)
    return jnp.concatenate([jnp.cos(angles) * factor, -jnp.sin(angles) * factor], 0).astype(jnp.bfloat16)

def smoothing_matrix():
    rows = jnp.arange(F + 2 * HALF, dtype=jnp.int32)[:, None]
    cols = jnp.arange(F, dtype=jnp.int32)[None, :]
    inside = jnp.abs(rows - cols - HALF) <= HALF
    return jnp.where(inside, 1.0 / (2 * HALF + 1), 0.0).astype(jnp.float32)

def band_weights():
    freqs = jnp.arange(F, dtype=jnp.int32).astype(jnp.float32) + 0.5
    edge_ramp = jnp.minimum(freqs, F - freqs) / (F / 4.0)
    return jnp.where(edge_ramp < 1.0, 0.5 - 0.5 * jnp.cos(math.pi * edge_ramp), 1.0).astype(jnp.float32)

def whiten(block, live_rows, forward, smoother, band_taper):
    raw_spec = jnp.einsum('wnc,nk->wck', block.astype(jnp.float32), forward.astype(jnp.float32))
    width = F + 2 * HALF
    real_part = raw_spec[..., :width]
    imag_part = raw_spec[..., width:]
    magnitude = jnp.sqrt(real_part * real_part + imag_part * imag_part)
    smooth = jnp.dot(magnitude, smoother, precision=lax.Precision.HIGHEST)
    weighting = band_taper[None, None, :] * live_rows.astype(jnp.float32)[None, :, None] / (smooth + whiten_eps)
    return jnp.concatenate([real_part[..., HALF:HALF + F] * weighting, imag_part[..., HALF:HALF + F] * weighting], -1).astype(jnp.bfloat16)

def cross_spectrum(left_block, right_block):
    left_all = left_block.astype(jnp.float32)
    right_all = right_block.astype(jnp.float32)
    left_real, left_imag = (left_all[..., :F], left_all[..., F:])
    right_real, right_imag = (right_all[..., :F], right_all[..., F:])
    real_sum = jnp.einsum('wif,wjf->ijf', left_real, right_real) + jnp.einsum('wif,wjf->ijf', left_imag, right_imag)
    imag_sum = jnp.einsum('wif,wjf->ijf', left_imag, right_real) - jnp.einsum('wif,wjf->ijf', left_real, right_imag)
    return jnp.concatenate([real_sum, imag_sum], -1).reshape(CB * CB, 2 * F).astype(jnp.bfloat16)

def reference(strain, live_mask, block_pairs):
    forward = forward_table()
    smoother = smoothing_matrix()
    band_taper = band_weights()
    backward = backward_table()
    blocks = strain.reshape(N_TM * WIN_DEV, W, N_CHAN, CB).transpose(2, 0, 1, 3)
    live_rows = live_mask.reshape(N_CHAN, CB)
    spectra = lax.map(lambda operand_pair: whiten(operand_pair[0], operand_pair[1], forward, smoother, band_taper), (blocks, live_rows))
    spectra = spectra.transpose(1, 0, 2, 3).reshape(N_TM, WIN_DEV, N_CHAN * CB, 2 * F)
    flat_pairs = block_pairs.reshape(-1, 2)

    def correlate(block_pair):
        summed = jnp.zeros((CB * CB, LAGS), jnp.float32)
        for group in range(N_TM):
            left_block = lax.dynamic_slice_in_dim(spectra[group], (block_pair[0] * CB).astype(jnp.int32), CB, 1)
            right_block = lax.dynamic_slice_in_dim(spectra[group], (block_pair[1] * CB).astype(jnp.int32), CB, 1)
            cross_spec = cross_spectrum(left_block, right_block)
            partial_value = jnp.dot(cross_spec, backward, preferred_element_type=jnp.float32).astype(jnp.bfloat16)
            partial_value = lax.optimization_barrier(partial_value)
            summed = summed + partial_value.astype(jnp.float32)
        return summed.astype(jnp.bfloat16).reshape(CB, CB, LAGS)
    result = lax.map(correlate, flat_pairs)
    return result.reshape(N_TM, N_CHAN * PAIRS_HALF, CB, CB, LAGS)
```

```python
import functools
import math

import jax
import jax.numpy as jnp
import numpy as np
from jax import lax
from jax.experimental import pallas as pl
from jax.experimental.pallas import tpu as pltpu
from jax.sharding import PartitionSpec as P

CB = 64
W = 16000
NB = 64
WIN_DEV = 3
NWIN = 6
K0 = 64
F = 256
HALF = 32
WIDTH = F + 2 * HALF
LAGS = 1024
SAMPLES = W // NB
RANK = 24
UNITS = 5
ROWS = 8 * UNITS
CHUNK = 24
LANES = 128
TILES = CB * NB // LANES
EPS = 1e-05
F32 = jnp.float32
BF16 = jnp.bfloat16


def time_basis():
    places = np.arange(SAMPLES)
    main = ((SAMPLES - 1 - 2 * places) / 2.0) ** 2 * np.cos(2 * np.pi * (K0 - HALF + WIDTH) / W)
    side = places[1:] * (SAMPLES - places[1:]) / 2.0
    _, vectors = np.linalg.eigh(np.diag(main) + np.diag(side, 1) + np.diag(side, -1))
    basis = vectors[:, ::-1][:, :RANK]
    mid = SAMPLES // 2
    centre = np.where(np.arange(RANK) % 2 == 0, basis[mid] + basis[mid - 1], basis[mid] - basis[mid - 1])
    return basis * np.sign(centre)[None, :]


def block_tables(basis):
    local = np.arange(SAMPLES)
    bins = np.arange(K0 - HALF, K0 - HALF + WIDTH)
    out = np.empty((2 * WIDTH, RANK // 8, NB, 8))
    for block in range(NB):
        index = ((block * SAMPLES + local)[:, None] * bins[None, :]) % W
        angles = 2 * np.pi / W * index
        table = np.concatenate([np.cos(angles), -np.sin(angles)], 1)
        out[:, :, block, :] = (table.T @ basis).reshape(2 * WIDTH, RANK // 8, 8)
    return out.reshape(2 * WIDTH, RANK * NB)


def lag_table():
    freqs = (K0 + np.arange(F))[:, None]
    steps = (np.arange(LAGS) - LAGS // 2)[None, :]
    angles = 2 * np.pi / W * (freqs * steps % W)
    factor = 1.0 / math.sqrt(WIN_DEV * F)
    return np.concatenate([np.cos(angles) * factor, -np.sin(angles) * factor], 0)


def smoothing_ones():
    rows = np.arange(F)[:, None]
    cols = np.arange(WIDTH)[None, :]
    return (np.abs(cols - rows - HALF) <= HALF).astype(np.float32)


def band_weights():
    freqs = np.arange(F) + 0.5
    ramp = np.minimum(freqs, F - freqs) / (F / 4.0)
    return np.where(ramp < 1.0, 0.5 - 0.5 * np.cos(np.pi * ramp), 1.0)


def project_kernel(steps, pairs_ref, live_ref, basis_ref, x_ref, o_ref, z_ref):
    step = pl.program_id(0)
    per = TILES // steps
    block = lax.axis_index("chan")
    place = lax.broadcasted_iota(jnp.int32, (1, SAMPLES), 1) + block * SAMPLES
    hann = 0.5 - 0.5 * jnp.cos((2.0 * math.pi / W) * place.astype(F32))
    table = (basis_ref[...] * hann).astype(BF16)
    for win in range(WIN_DEV):
        coef = jnp.dot(table, x_ref[win], preferred_element_type=F32)
        for tile in range(per):
            at = 2 * (step * per + tile)
            part = coef[:, tile * LANES : (tile + 1) * LANES]
            unit = [part[8 * s : 8 * s + 8] for s in range(3)]
            if win < 2:
                for s in range(3):
                    z_ref[s, at + win] = unit[s]
            else:
                z_ref[3, at] = unit[0]
                z_ref[3, at + 1] = unit[1]
                z_ref[4, at] = unit[2]
                z_ref[4, at + 1] = jnp.zeros((8, LANES), F32)

    @pl.when(step == steps - 1)
    def _():
        lane = lax.broadcasted_iota(jnp.int32, (8, LANES), 1)
        extra = jnp.zeros((8, LANES), F32)
        for s in range(2):
            for side in range(2):
                value = pairs_ref[s, 0, side].astype(F32)
                extra = jnp.where(lane == 1 + 4 * s + 2 * side, value, extra)
        for u in range(UNITS):
            z = [z_ref[u, v] for v in range(CB)]
            for bit in range(6):
                stride = 1 << bit
                high = ((lane >> bit) & 1) == 1
                for v in range(CB):
                    if v & stride:
                        continue
                    x0, x1 = z[v], z[v | stride]
                    z[v] = jnp.where(high, pltpu.roll(x1, stride, 1), x0)
                    z[v | stride] = jnp.where(high, x1, pltpu.roll(x0, LANES - stride, 1))
            if u == UNITS - 1:
                for v in range(CB):
                    z[v] = z[v] + jnp.where(lane == 9, live_ref[v].astype(F32), extra)
            for v in range(CB):
                z_ref[u, v] = z[v]
        for v in range(CB):
            o_ref[v] = jnp.concatenate([z_ref[u, v] for u in range(UNITS)], 0).astype(BF16)


def project(strain, live_mask, block_pairs, basis):
    steps = 4
    width = CB * NB // steps
    return pl.pallas_call(
        functools.partial(project_kernel, steps),
        grid=(steps,),
        out_shape=jax.ShapeDtypeStruct((CB, ROWS, LANES), BF16),
        in_specs=[
            pl.BlockSpec(memory_space=pltpu.SMEM),
            pl.BlockSpec(memory_space=pltpu.SMEM),
            pl.BlockSpec((RANK, SAMPLES), lambda g: (0, 0)),
            pl.BlockSpec((WIN_DEV, SAMPLES, width), lambda g: (0, 0, g)),
        ],
        out_specs=pl.BlockSpec((CB, ROWS, LANES), lambda g: (0, 0, 0)),
        scratch_shapes=[pltpu.VMEM((UNITS, CB, 8, LANES), F32)],
        compiler_params=pltpu.CompilerParams(vmem_limit_bytes=24 * 2**20),
        cost_estimate=pl.CostEstimate(flops=400_000_000, bytes_accessed=7_000_000, transcendentals=0),
        name="project",
    )(block_pairs, live_mask, basis, strain)


def slot(index):
    return ((index & 1) << 5) | (index >> 1)


def whiten_kernel(r_ref, table_ref, ones_ref, taper_ref, o_ref, extra_ref, index_ref, small_ref, spec_ref, rows_ref, sem):
    received = r_ref[...].astype(F32)
    unit = [received[:, 8 * u : 8 * u + 8].reshape(8 * NB, LANES) for u in range(UNITS)]
    extra_ref[...] = unit[4]
    index_ref[...] = extra_ref[pl.ds(0, NB, stride=8), :].astype(jnp.int32)
    copy = pltpu.make_async_copy(index_ref, small_ref, sem)
    copy.start()
    even = extra_ref[pl.ds(0, NB // 2, stride=16), :]
    odd = extra_ref[pl.ds(8, NB // 2, stride=16), :]
    live = jnp.concatenate([even, odd], 0)[:, 9:10]
    left = jnp.concatenate(unit[:3], 0)
    right = jnp.concatenate([unit[3], pltpu.roll(unit[3], LANES - 1, 1), unit[4]], 0)
    operand = jnp.concatenate([left, right], 1).astype(BF16)
    raw = jnp.dot(table_ref[...], operand, preferred_element_type=F32)
    real, imag = raw[:WIDTH], raw[WIDTH:]
    magnitude = jnp.sqrt(real * real + imag * imag)
    ones = ones_ref[...]
    total = jnp.zeros((F, 2 * LANES), F32)
    rest = magnitude
    for _ in range(3):
        piece = rest.astype(BF16)
        rest = rest - piece.astype(F32)
        total = total + jnp.dot(ones, piece, preferred_element_type=F32)
    weight = 1.0 / (total * (1.0 / (2 * HALF + 1)) + EPS)
    for tile in range(2 * F // LANES):
        part = real if tile < F // LANES else imag
        start = tile * LANES % F
        picked = part[HALF + start : HALF + start + LANES] * weight[start : start + LANES]
        spec_ref[tile] = picked.T
    for win, start in enumerate((0, 1, LANES)):
        for tile in range(2 * F // LANES):
            cols = slice(tile * LANES, (tile + 1) * LANES)
            value = spec_ref[tile, pl.ds(start, NB, stride=2), :] * taper_ref[:, cols] * live
            rows_ref[pl.ds(win * 4 + tile, NB, stride=16), :] = value
            if win == 2:
                rows_ref[pl.ds(12 + tile, NB, stride=16), :] = value
    copy.wait()
    low = lax.broadcasted_iota(jnp.int32, (8, LANES), 0) < 4

    @pl.loop(0, NB)
    def _(device):
        for s in range(2):
            first = slot(small_ref[device, 1 + 4 * s])
            second = slot(small_ref[device, 3 + 4 * s])
            a = rows_ref[pl.ds(pl.multiple_of(first * 16, 16), 16), :]
            b = rows_ref[pl.ds(pl.multiple_of(second * 16, 16), 16), :]
            chunk = jnp.concatenate([a[:8], jnp.where(low, a[8:], b[8:]), b[:8]], 0)
            o_ref[s * NB + device] = chunk.astype(BF16)


def whiten(received, table, ones, taper):
    return pl.pallas_call(
        whiten_kernel,
        out_shape=jax.ShapeDtypeStruct((2 * NB, CHUNK, LANES), BF16),
        in_specs=[pl.BlockSpec(memory_space=pltpu.VMEM)] * 4,
        out_specs=pl.BlockSpec(memory_space=pltpu.VMEM),
        scratch_shapes=[
            pltpu.VMEM((8 * NB, LANES), F32),
            pltpu.VMEM((NB, LANES), jnp.int32),
            pltpu.SMEM((NB, LANES), jnp.int32),
            pltpu.VMEM((2 * F // LANES, 2 * LANES, LANES), F32),
            pltpu.VMEM((16 * NB, LANES), F32),
            pltpu.SemaphoreType.DMA,
        ],
        compiler_params=pltpu.CompilerParams(vmem_limit_bytes=24 * 2**20),
        cost_estimate=pl.CostEstimate(flops=600_000_000, bytes_accessed=4_000_000, transcendentals=100_000),
        name="whiten",
    )(received, table, ones, taper)


GROUP = 8


def lags_kernel(g_ref, back_ref, o_ref, flat_ref, a_ref, b_ref, cross_ref):
    step = pl.program_id(0)

    @pl.when(step == 0)
    def _():
        flat_ref[...] = g_ref[...].astype(F32).reshape(2 * CB * CHUNK, LANES)
        for group in range(2):
            for win in range(WIN_DEV):
                for tile in range(2 * F // LANES):
                    cols = slice(tile * LANES, (tile + 1) * LANES)
                    at = win * 4 + tile
                    places = (at, 12 + tile if win == 2 else 16 + at)
                    for ref, place in zip((a_ref, b_ref), places):
                        start = group * CB * CHUNK + place
                        ref[group * WIN_DEV + win, :, cols] = flat_ref[pl.ds(start, CB, stride=CHUNK), :]

    rows = pl.ds(pl.multiple_of(step * GROUP, GROUP), GROUP)
    for k in range(GROUP):
        for tile in range(F // LANES):
            re = slice(tile * LANES, (tile + 1) * LANES)
            im = slice(F + tile * LANES, F + (tile + 1) * LANES)
            real = jnp.zeros((CB, LANES), F32)
            imag = jnp.zeros((CB, LANES), F32)
            for win in range(NWIN):
                ar = a_ref[win, rows, re][k : k + 1]
                ai = a_ref[win, rows, im][k : k + 1]
                br = b_ref[win, :, re]
                bi = b_ref[win, :, im]
                real = real + (ar * br + ai * bi)
                imag = imag + (ai * br - ar * bi)
            cross_ref[k * CB : (k + 1) * CB, re] = real.astype(BF16)
            cross_ref[k * CB : (k + 1) * CB, im] = imag.astype(BF16)
    lags = jnp.dot(cross_ref[...], back_ref[...], preferred_element_type=F32)
    o_ref[...] = lags.astype(BF16).reshape(GROUP, CB, LAGS)


def pair_lags(gathered, back):
    return pl.pallas_call(
        lags_kernel,
        grid=(CB // GROUP,),
        out_shape=jax.ShapeDtypeStruct((CB, CB, LAGS), BF16),
        in_specs=[
            pl.BlockSpec((2 * CB, CHUNK, LANES), lambda g: (0, 0, 0)),
            pl.BlockSpec((2 * F, LAGS), lambda g: (0, 0)),
        ],
        out_specs=pl.BlockSpec((GROUP, CB, LAGS), lambda g: (g, 0, 0)),
        scratch_shapes=[
            pltpu.VMEM((2 * CB * CHUNK, LANES), F32),
            pltpu.VMEM((NWIN, CB, 2 * F), F32),
            pltpu.VMEM((NWIN, CB, 2 * F), F32),
            pltpu.VMEM((GROUP * CB, 2 * F), BF16),
        ],
        compiler_params=pltpu.CompilerParams(vmem_limit_bytes=32 * 2**20),
        cost_estimate=pl.CostEstimate(flops=4_400_000_000, bytes_accessed=12_000_000, transcendentals=0),
        name="pair_lags",
    )(gathered, back)


def solution(mesh):
    basis_np = time_basis()
    table_np = block_tables(basis_np).astype(jnp.bfloat16)
    back_np = lag_table().astype(jnp.bfloat16)

    def per_device(strain, live_mask, block_pairs):
        basis = jnp.asarray(basis_np.T.astype(np.float32))
        ones = jnp.asarray(smoothing_ones().astype(jnp.bfloat16))
        taper = jnp.asarray(np.tile(band_weights(), 2)[None, :].astype(np.float32))
        coefs = project(strain, live_mask, block_pairs, basis)
        with jax.named_scope("channels_exchange"):
            received = lax.all_to_all(coefs, "chan", 0, 0, tiled=True)
        chosen = whiten(received, jnp.asarray(table_np), ones, taper)
        with jax.named_scope("pairs_exchange"):
            gathered = lax.all_to_all(chosen, ("tm", "chan"), 0, 0, tiled=True)
        return pair_lags(gathered, jnp.asarray(back_np)).reshape(1, 1, CB, CB, LAGS)

    in_specs = (P("tm", "chan", None), P("chan"), P(None, "chan", None))
    out_specs = P("tm", "chan", None, None, None)
    return jax.shard_map(per_device, mesh=mesh, in_specs=in_specs, out_specs=out_specs, check_vma=False)
```

```python
import functools
import math

import jax
import jax.numpy as jnp
import numpy as np
from jax import lax
from jax.experimental import pallas as pl
from jax.experimental.pallas import tpu as pltpu
from jax.sharding import PartitionSpec as P

CB = 64
W = 16000
NB = 64
WIN_DEV = 3
NWIN = 6
K0 = 64
F = 256
HALF = 32
WIDTH = F + 2 * HALF
LAGS = 1024
SAMPLES = W // NB
RANK = 24
UNITS = 5
ROWS = 8 * UNITS
CHUNK = 24
LANES = 128
TILES = CB * NB // LANES
EPS = 1e-05
F32 = jnp.float32
BF16 = jnp.bfloat16


def time_basis():
    places = np.arange(SAMPLES)
    main = ((SAMPLES - 1 - 2 * places) / 2.0) ** 2 * np.cos(2 * np.pi * (K0 - HALF + WIDTH) / W)
    side = places[1:] * (SAMPLES - places[1:]) / 2.0
    _, vectors = np.linalg.eigh(np.diag(main) + np.diag(side, 1) + np.diag(side, -1))
    basis = vectors[:, ::-1][:, :RANK]
    mid = SAMPLES // 2
    centre = np.where(np.arange(RANK) % 2 == 0, basis[mid] + basis[mid - 1], basis[mid] - basis[mid - 1])
    return basis * np.sign(centre)[None, :]


def block_tables(basis):
    local = np.arange(SAMPLES)
    bins = np.arange(K0 - HALF, K0 - HALF + WIDTH)
    out = np.empty((2 * WIDTH, RANK // 8, NB, 8))
    for block in range(NB):
        index = ((block * SAMPLES + local)[:, None] * bins[None, :]) % W
        angles = 2 * np.pi / W * index
        table = np.concatenate([np.cos(angles), -np.sin(angles)], 1)
        out[:, :, block, :] = (table.T @ basis).reshape(2 * WIDTH, RANK // 8, 8)
    return out.reshape(2 * WIDTH, RANK * NB)


def lag_table():
    freqs = (K0 + np.arange(F))[:, None]
    steps = (np.arange(LAGS) - LAGS // 2)[None, :]
    angles = 2 * np.pi / W * (freqs * steps % W)
    factor = 1.0 / math.sqrt(WIN_DEV * F)
    return np.concatenate([np.cos(angles) * factor, -np.sin(angles) * factor], 0)


def smoothing_ones():
    rows = np.arange(F)[:, None]
    cols = np.arange(WIDTH)[None, :]
    return (np.abs(cols - rows - HALF) <= HALF).astype(np.float32)


def band_weights():
    freqs = np.arange(F) + 0.5
    ramp = np.minimum(freqs, F - freqs) / (F / 4.0)
    return np.where(ramp < 1.0, 0.5 - 0.5 * np.cos(np.pi * ramp), 1.0)


def project_kernel(parts, pairs_hbm, live_hbm, basis_ref, x_hbm, o_ref, x_ref, z_ref, pairs_ref, live_ref, sems):
    per = TILES // parts
    width = CB * NB // parts
    copies = []
    for c in range(parts):
        cols = pl.ds(c * width, width)
        copies.append(pltpu.make_async_copy(x_hbm.at[:, :, cols], x_ref.at[:, :, cols], sems.at[c]))
    small = [
        pltpu.make_async_copy(pairs_hbm, pairs_ref, sems.at[parts]),
        pltpu.make_async_copy(live_hbm, live_ref, sems.at[parts + 1]),
    ]
    for copy in copies + small:
        copy.start()
    block = lax.axis_index("chan")
    place = lax.broadcasted_iota(jnp.int32, (1, SAMPLES), 1) + block * SAMPLES
    hann = 0.5 - 0.5 * jnp.cos((2.0 * math.pi / W) * place.astype(F32))
    table = (basis_ref[...] * hann).astype(BF16)
    lane = lax.broadcasted_iota(jnp.int32, (16, LANES), 1)
    masks = [((lane >> bit) & 1) == 1 for bit in range(6)]

    def exchange(groups, bits, base):
        for bit in bits:
            stride, shift = 1 << (bit - base), 1 << bit
            for v in range(len(groups[0])):
                if v & stride:
                    continue
                for z in groups:
                    x0, x1 = z[v], z[v | stride]
                    z[v] = jnp.where(masks[bit], pltpu.roll(x1, shift, 1), x0)
                    z[v | stride] = jnp.where(masks[bit], x1, pltpu.roll(x0, LANES - shift, 1))

    count = 2 * per
    local = count.bit_length() - 1
    zero = jnp.zeros((8, LANES), BF16)
    for c in range(parts):
        copies[c].wait()
        coef = [
            jnp.dot(table, x_ref[win, :, c * width : (c + 1) * width], preferred_element_type=F32).astype(BF16)
            for win in range(WIN_DEV)
        ]
        groups = [[], [], []]
        for tile in range(per):
            part = [coef[win][:, tile * LANES : (tile + 1) * LANES] for win in range(WIN_DEV)]
            for h in range(2):
                groups[0].append(part[h][:16])
                groups[1].append(jnp.concatenate([part[h][16:], part[2][8 * h : 8 * h + 8]], 0))
                groups[2].append(jnp.concatenate([part[2][16:] if h == 0 else zero, zero], 0))
        exchange(groups, range(local), 0)
        for k in range(3):
            for v in range(count):
                z_ref[k, c * count + v] = groups[k][v]
    for copy in small:
        copy.wait()
    lane = lax.broadcasted_iota(jnp.int32, (8, LANES), 1)
    extra = jnp.zeros((8, LANES), F32)
    for s in range(2):
        for side in range(2):
            value = pairs_ref[s, 0, side].astype(F32)
            extra = jnp.where(lane == 1 + 4 * s + 2 * side, value, extra)
    for first in range(0, count, 4):
        groups = [[z_ref[k, v + count * c] for c in range(parts)] for k in range(3) for v in range(first, first + 4)]
        exchange(groups, range(local, 6), local)
        for k in range(3):
            for v in range(4):
                for c in range(parts):
                    slab = first + v + count * c
                    value = groups[k * 4 + v][c]
                    if k < 2:
                        o_ref[slab, 16 * k : 16 * k + 16] = value
                    else:
                        added = jnp.where(lane == 9, live_ref[slab].astype(F32), extra)
                        o_ref[slab, 32:40] = (value[:8].astype(F32) + added).astype(BF16)


def project(strain, live_mask, block_pairs, basis):
    parts = 2
    return pl.pallas_call(
        functools.partial(project_kernel, parts),
        out_shape=jax.ShapeDtypeStruct((CB, ROWS, LANES), BF16),
        in_specs=[
            pl.BlockSpec(memory_space=pltpu.HBM),
            pl.BlockSpec(memory_space=pltpu.HBM),
            pl.BlockSpec(memory_space=pltpu.VMEM),
            pl.BlockSpec(memory_space=pltpu.HBM),
        ],
        out_specs=pl.BlockSpec(memory_space=pltpu.VMEM),
        scratch_shapes=[
            pltpu.VMEM((WIN_DEV, SAMPLES, CB * NB), BF16),
            pltpu.VMEM((3, CB, 16, LANES), BF16),
            pltpu.SMEM((2, 1, 2), jnp.int32),
            pltpu.SMEM((CB,), jnp.int32),
            pltpu.SemaphoreType.DMA((parts + 2,)),
        ],
        compiler_params=pltpu.CompilerParams(vmem_limit_bytes=58 * 2**20),
        cost_estimate=pl.CostEstimate(flops=400_000_000, bytes_accessed=7_000_000, transcendentals=0),
        name="project",
    )(block_pairs, live_mask, basis, strain)


def slot(index):
    return ((index & 1) << 5) | (index >> 1)


def whiten_kernel(r_ref, table_ref, ones_ref, taper_ref, o_ref, extra_ref, index_ref, small_ref, spec_ref, rows_ref, sem):
    received = r_ref[...].astype(F32)
    unit = [received[:, 8 * u : 8 * u + 8].reshape(8 * NB, LANES) for u in range(UNITS)]
    extra_ref[...] = unit[4]
    index_ref[...] = extra_ref[pl.ds(0, NB, stride=8), :].astype(jnp.int32)
    copy = pltpu.make_async_copy(index_ref, small_ref, sem)
    copy.start()
    even = extra_ref[pl.ds(0, NB // 2, stride=16), :]
    odd = extra_ref[pl.ds(8, NB // 2, stride=16), :]
    live = jnp.concatenate([even, odd], 0)[:, 9:10]
    left = jnp.concatenate(unit[:3], 0)
    right = jnp.concatenate([unit[3], pltpu.roll(unit[3], LANES - 1, 1), unit[4]], 0)
    operand = jnp.concatenate([left, right], 1).astype(BF16)
    raw = jnp.dot(table_ref[...], operand, preferred_element_type=F32)
    real, imag = raw[:WIDTH], raw[WIDTH:]
    magnitude = jnp.sqrt(real * real + imag * imag)
    ones = ones_ref[...]
    total = jnp.zeros((F, 2 * LANES), F32)
    rest = magnitude
    for _ in range(3):
        piece = rest.astype(BF16)
        rest = rest - piece.astype(F32)
        total = total + jnp.dot(ones, piece, preferred_element_type=F32)
    weight = 1.0 / (total * (1.0 / (2 * HALF + 1)) + EPS)
    for tile in range(2 * F // LANES):
        part = real if tile < F // LANES else imag
        start = tile * LANES % F
        picked = part[HALF + start : HALF + start + LANES] * weight[start : start + LANES]
        spec_ref[tile] = picked.T
    for win, start in enumerate((0, 1, LANES)):
        for tile in range(2 * F // LANES):
            cols = slice(tile * LANES, (tile + 1) * LANES)
            value = spec_ref[tile, pl.ds(start, NB, stride=2), :] * taper_ref[:, cols] * live
            rows_ref[pl.ds(win * 4 + tile, NB, stride=16), :] = value
            if win == 2:
                rows_ref[pl.ds(12 + tile, NB, stride=16), :] = value
    copy.wait()
    low = lax.broadcasted_iota(jnp.int32, (8, LANES), 0) < 4

    @pl.loop(0, NB, unroll=8)
    def _(device):
        for s in range(2):
            first = slot(small_ref[device, 1 + 4 * s])
            second = slot(small_ref[device, 3 + 4 * s])
            a = rows_ref[pl.ds(pl.multiple_of(first * 16, 16), 16), :]
            b = rows_ref[pl.ds(pl.multiple_of(second * 16, 16), 16), :]
            chunk = jnp.concatenate([a[:8], jnp.where(low, a[8:], b[8:]), b[:8]], 0)
            o_ref[s * NB + device] = chunk.astype(BF16)


def whiten(received, table, ones, taper):
    return pl.pallas_call(
        whiten_kernel,
        out_shape=jax.ShapeDtypeStruct((2 * NB, CHUNK, LANES), BF16),
        in_specs=[pl.BlockSpec(memory_space=pltpu.VMEM)] * 4,
        out_specs=pl.BlockSpec(memory_space=pltpu.VMEM),
        scratch_shapes=[
            pltpu.VMEM((8 * NB, LANES), F32),
            pltpu.VMEM((NB, LANES), jnp.int32),
            pltpu.SMEM((NB, LANES), jnp.int32),
            pltpu.VMEM((2 * F // LANES, 2 * LANES, LANES), F32),
            pltpu.VMEM((16 * NB, LANES), F32),
            pltpu.SemaphoreType.DMA,
        ],
        compiler_params=pltpu.CompilerParams(vmem_limit_bytes=24 * 2**20),
        cost_estimate=pl.CostEstimate(flops=600_000_000, bytes_accessed=4_000_000, transcendentals=100_000),
        name="whiten",
    )(received, table, ones, taper)


GROUP = 16


def lags_kernel(g_ref, back_ref, o_ref, flat_ref, a_ref, b_ref, cross_ref):
    step = pl.program_id(0)

    @pl.when(step == 0)
    def _():
        flat_ref[...] = g_ref[...].astype(F32).reshape(2 * CB * CHUNK, LANES)
        for group in range(2):
            for win in range(WIN_DEV):
                for tile in range(2 * F // LANES):
                    cols = slice(tile * LANES, (tile + 1) * LANES)
                    at = win * 4 + tile
                    places = (at, 12 + tile if win == 2 else 16 + at)
                    for ref, place in zip((a_ref, b_ref), places):
                        start = group * CB * CHUNK + place
                        value = flat_ref[pl.ds(start, CB, stride=CHUNK), :]
                        ref[group * WIN_DEV + win, :, cols] = value.astype(ref.dtype)

    rows = pl.ds(pl.multiple_of(step * GROUP, GROUP), GROUP)

    def spread(value):
        value = jnp.broadcast_to(value, (16, LANES)).astype(BF16)
        return jnp.concatenate([value] * (CB // 16), 0)

    def total(terms):
        return ((terms[0] + terms[1]) + (terms[2] + terms[3])) + (terms[4] + terms[5])

    for k in range(GROUP):
        for tile in range(F // LANES):
            re = slice(tile * LANES, (tile + 1) * LANES)
            im = slice(F + tile * LANES, F + (tile + 1) * LANES)
            real, imag = [], []
            for win in range(NWIN):
                ar = spread(a_ref[win, rows, re][k : k + 1])
                ai = spread(a_ref[win, rows, im][k : k + 1])
                br = b_ref[win, :, re]
                bi = b_ref[win, :, im]
                real.append(ar * br + ai * bi)
                imag.append(ai * br - ar * bi)
            cross_ref[k * CB : (k + 1) * CB, re] = total(real)
            cross_ref[k * CB : (k + 1) * CB, im] = total(imag)
    lags = jnp.dot(cross_ref[...], back_ref[...], preferred_element_type=F32)
    o_ref[...] = lags.astype(BF16).reshape(GROUP, CB, LAGS)


def pair_lags(gathered, back):
    return pl.pallas_call(
        lags_kernel,
        grid=(CB // GROUP,),
        out_shape=jax.ShapeDtypeStruct((CB, CB, LAGS), BF16),
        in_specs=[pl.BlockSpec(memory_space=pltpu.VMEM)] * 2,
        out_specs=pl.BlockSpec((GROUP, CB, LAGS), lambda g: (g, 0, 0)),
        scratch_shapes=[
            pltpu.VMEM((2 * CB * CHUNK, LANES), F32),
            pltpu.VMEM((NWIN, CB, 2 * F), F32),
            pltpu.VMEM((NWIN, CB, 2 * F), BF16),
            pltpu.VMEM((GROUP * CB, 2 * F), BF16),
        ],
        compiler_params=pltpu.CompilerParams(vmem_limit_bytes=32 * 2**20),
        cost_estimate=pl.CostEstimate(flops=4_400_000_000, bytes_accessed=12_000_000, transcendentals=0),
        name="pair_lags",
    )(gathered, back)


def solution(mesh):
    basis_np = time_basis()
    table_np = block_tables(basis_np).astype(jnp.bfloat16)
    back_np = lag_table().astype(jnp.bfloat16)

    def per_device(strain, live_mask, block_pairs):
        basis = jnp.asarray(basis_np.T.astype(np.float32))
        ones = jnp.asarray(smoothing_ones().astype(jnp.bfloat16))
        taper = jnp.asarray(np.tile(band_weights(), 2)[None, :].astype(np.float32))
        coefs = project(strain, live_mask, block_pairs, basis)
        with jax.named_scope("channels_exchange"):
            received = lax.all_to_all(coefs, "chan", 0, 0, tiled=True)
        chosen = whiten(received, jnp.asarray(table_np), ones, taper)
        with jax.named_scope("pairs_exchange"):
            gathered = lax.all_to_all(chosen, ("tm", "chan"), 0, 0, tiled=True)
        return pair_lags(gathered, jnp.asarray(back_np)).reshape(1, 1, CB, CB, LAGS)

    in_specs = (P("tm", "chan", None), P("chan"), P(None, "chan", None))
    out_specs = P("tm", "chan", None, None, None)
    return jax.shard_map(per_device, mesh=mesh, in_specs=in_specs, out_specs=out_specs, check_vma=False)
```

```python
import functools
import math

import jax
import jax.numpy as jnp
import numpy as np
from jax import lax
from jax.experimental import pallas as pl
from jax.experimental.pallas import tpu as pltpu
from jax.sharding import PartitionSpec as P

CB = 64
W = 16000
NB = 64
WIN_DEV = 3
NWIN = 6
K0 = 64
F = 256
HALF = 32
WIDTH = F + 2 * HALF
LAGS = 1024
SAMPLES = W // NB
RANK = 24
UNITS = 5
ROWS = 8 * UNITS
CHUNK = 24
LANES = 128
TILES = CB * NB // LANES
EPS = 1e-05
F32 = jnp.float32
BF16 = jnp.bfloat16


def time_basis():
    places = np.arange(SAMPLES)
    main = ((SAMPLES - 1 - 2 * places) / 2.0) ** 2 * np.cos(2 * np.pi * (K0 - HALF + WIDTH) / W)
    side = places[1:] * (SAMPLES - places[1:]) / 2.0
    _, vectors = np.linalg.eigh(np.diag(main) + np.diag(side, 1) + np.diag(side, -1))
    basis = vectors[:, ::-1][:, :RANK]
    mid = SAMPLES // 2
    centre = np.where(np.arange(RANK) % 2 == 0, basis[mid] + basis[mid - 1], basis[mid] - basis[mid - 1])
    return basis * np.sign(centre)[None, :]


def block_tables(basis):
    local = np.arange(SAMPLES)
    bins = np.arange(K0 - HALF, K0 - HALF + WIDTH)
    out = np.empty((2 * WIDTH, RANK // 8, NB, 8))
    for block in range(NB):
        index = ((block * SAMPLES + local)[:, None] * bins[None, :]) % W
        angles = 2 * np.pi / W * index
        table = np.concatenate([np.cos(angles), -np.sin(angles)], 1)
        out[:, :, block, :] = (table.T @ basis).reshape(2 * WIDTH, RANK // 8, 8)
    return out.reshape(2 * WIDTH, RANK * NB)


def lag_table():
    freqs = (K0 + np.arange(F))[:, None]
    steps = (np.arange(LAGS) - LAGS // 2)[None, :]
    angles = 2 * np.pi / W * (freqs * steps % W)
    factor = 1.0 / math.sqrt(WIN_DEV * F)
    return np.concatenate([np.cos(angles) * factor, -np.sin(angles) * factor], 0)


def smoothing_ones():
    rows = np.arange(F)[:, None]
    cols = np.arange(WIDTH)[None, :]
    return (np.abs(cols - rows - HALF) <= HALF).astype(np.float32)


def band_weights():
    freqs = np.arange(F) + 0.5
    ramp = np.minimum(freqs, F - freqs) / (F / 4.0)
    return np.where(ramp < 1.0, 0.5 - 0.5 * np.cos(np.pi * ramp), 1.0)


def project_kernel(parts, pairs_hbm, live_hbm, basis_ref, x_hbm, o_ref, x_ref, z_ref, pairs_ref, live_ref, sems):
    per = TILES // parts
    width = CB * NB // parts
    copies = []
    for c in range(parts):
        cols = pl.ds(c * width, width)
        copies.append(pltpu.make_async_copy(x_hbm.at[:, :, cols], x_ref.at[:, :, cols], sems.at[c]))
    small = [
        pltpu.make_async_copy(pairs_hbm, pairs_ref, sems.at[parts]),
        pltpu.make_async_copy(live_hbm, live_ref, sems.at[parts + 1]),
    ]
    for copy in copies + small:
        copy.start()
    block = lax.axis_index("chan")
    place = lax.broadcasted_iota(jnp.int32, (1, SAMPLES), 1) + block * SAMPLES
    hann = 0.5 - 0.5 * jnp.cos((2.0 * math.pi / W) * place.astype(F32))
    table = (basis_ref[...] * hann).astype(BF16)
    lane = lax.broadcasted_iota(jnp.int32, (16, LANES), 1)
    masks = [((lane >> bit) & 1) == 1 for bit in range(6)]

    def exchange(groups, bits, base):
        for bit in bits:
            stride = 1 << (bit - base)
            for v in range(len(groups[0])):
                if v & stride:
                    continue
                for z in groups:
                    x0, x1 = z[v], z[v | stride]
                    if bit:
                        z[v] = jnp.where(masks[bit], x1, x0)
                        z[v | stride] = jnp.where(masks[bit], x0, x1)
                    else:
                        z[v] = jnp.where(masks[0], pltpu.roll(x1, 1, 1), x0)
                        z[v | stride] = jnp.where(masks[0], x1, pltpu.roll(x0, LANES - 1, 1))

    count = 2 * per
    local = count.bit_length() - 1
    zero = jnp.zeros((8, LANES), BF16)
    for c in range(parts):
        copies[c].wait()
        coef = [
            jnp.dot(table, x_ref[win, :, c * width : (c + 1) * width], preferred_element_type=F32).astype(BF16)
            for win in range(WIN_DEV)
        ]
        groups = [[], [], []]
        for tile in range(per):
            part = [coef[win][:, tile * LANES : (tile + 1) * LANES] for win in range(WIN_DEV)]
            for h in range(2):
                groups[0].append(part[h][:16])
                groups[1].append(jnp.concatenate([part[h][16:], part[2][8 * h : 8 * h + 8]], 0))
                groups[2].append(jnp.concatenate([part[2][16:] if h == 0 else zero, zero], 0))
        exchange(groups, range(local), 0)
        for k in range(3):
            for v in range(count):
                z_ref[k, c * count + v] = groups[k][v]
    for copy in small:
        copy.wait()
    lane = lax.broadcasted_iota(jnp.int32, (8, LANES), 1)
    even = block & (NB - 2)
    extra = jnp.zeros((8, LANES), F32)
    for s in range(2):
        for side in range(2):
            value = pairs_ref[s, 0, side].astype(F32)
            extra = jnp.where(lane == 1 + 4 * s + 2 * side, value, extra)
    for first in range(0, count, 4):
        groups = [[z_ref[k, v + count * c] for c in range(parts)] for k in range(3) for v in range(first, first + 4)]
        exchange(groups, range(local, 6), local)
        for k in range(3):
            for v in range(4):
                for c in range(parts):
                    slab = first + v + count * c
                    value = groups[k * 4 + v][c]
                    if k < 2:
                        o_ref[slab, 16 * k : 16 * k + 16] = value
                    else:
                        added = jnp.where(lane == 9, live_ref[slab ^ even].astype(F32), extra)
                        o_ref[slab, 32:40] = (value[:8].astype(F32) + added).astype(BF16)


def project(strain, live_mask, block_pairs, basis):
    parts = 2
    return pl.pallas_call(
        functools.partial(project_kernel, parts),
        out_shape=jax.ShapeDtypeStruct((CB, ROWS, LANES), BF16),
        in_specs=[
            pl.BlockSpec(memory_space=pltpu.HBM),
            pl.BlockSpec(memory_space=pltpu.HBM),
            pl.BlockSpec(memory_space=pltpu.VMEM),
            pl.BlockSpec(memory_space=pltpu.HBM),
        ],
        out_specs=pl.BlockSpec(memory_space=pltpu.VMEM),
        scratch_shapes=[
            pltpu.VMEM((WIN_DEV, SAMPLES, CB * NB), BF16),
            pltpu.VMEM((3, CB, 16, LANES), BF16),
            pltpu.SMEM((2, 1, 2), jnp.int32),
            pltpu.SMEM((CB,), jnp.int32),
            pltpu.SemaphoreType.DMA((parts + 2,)),
        ],
        compiler_params=pltpu.CompilerParams(vmem_limit_bytes=58 * 2**20),
        cost_estimate=pl.CostEstimate(flops=400_000_000, bytes_accessed=7_000_000, transcendentals=0),
        name="project",
    )(block_pairs, live_mask, basis, strain)


def slot(index, device):
    return ((index & 1) << 5) | ((index ^ device) >> 1)


def whiten_kernel(r_ref, table_ref, ones_ref, taper_ref, o_ref, extra_ref, index_ref, small_ref, spec_ref, rows_ref, sem):
    me = lax.axis_index("chan")
    received = r_ref[...].astype(F32)
    unit = [received[:, 8 * u : 8 * u + 8].reshape(8 * NB, LANES) for u in range(UNITS)]
    extra_ref[...] = unit[4]
    extra = extra_ref[pl.ds(0, NB, stride=8), :]
    index_ref[...] = slot(extra.astype(jnp.int32) & (NB - 1), me) * 16
    copy = pltpu.make_async_copy(index_ref, small_ref, sem)
    copy.start()
    place = lax.broadcasted_iota(jnp.int32, (NB, NB), 0)
    wanted = slot(lax.broadcasted_iota(jnp.int32, (NB, NB), 1), me)
    order = jnp.where(place == wanted, 1.0, 0.0).astype(BF16)
    live = jnp.dot(order, extra.astype(BF16), preferred_element_type=F32)[:, 9:10]
    left = jnp.concatenate(unit[:3], 0)
    right = jnp.concatenate([unit[3], pltpu.roll(unit[3], LANES - 1, 1), unit[4]], 0)
    operand = jnp.concatenate([left, right], 1).astype(BF16)
    raw = jnp.dot(table_ref[...], operand, preferred_element_type=F32)
    real, imag = raw[:WIDTH], raw[WIDTH:]
    magnitude = jnp.sqrt(real * real + imag * imag)
    ones = ones_ref[...]
    total = jnp.zeros((F, 2 * LANES), F32)
    rest = magnitude
    for _ in range(2):
        piece = rest.astype(BF16)
        rest = rest - piece.astype(F32)
        total = total + jnp.dot(ones, piece, preferred_element_type=F32)
    weight = 1.0 / (total * (1.0 / (2 * HALF + 1)) + EPS)
    for tile in range(2 * F // LANES):
        part = real if tile < F // LANES else imag
        start = tile * LANES % F
        picked = part[HALF + start : HALF + start + LANES] * weight[start : start + LANES]
        spec_ref[tile] = picked.T
    for win, start in enumerate((0, 1, LANES)):
        for tile in range(2 * F // LANES):
            cols = slice(tile * LANES, (tile + 1) * LANES)
            value = spec_ref[tile, pl.ds(start, NB, stride=2), :] * taper_ref[:, cols] * live
            rows_ref[pl.ds(win * 4 + tile, NB, stride=16), :] = value
            if win == 2:
                rows_ref[pl.ds(12 + tile, NB, stride=16), :] = value
    copy.wait()
    low = lax.broadcasted_iota(jnp.int32, (8, LANES), 0) < 4

    @pl.loop(0, NB, unroll=8)
    def _(device):
        for s in range(2):
            first = pl.multiple_of(small_ref[device, 1 + 4 * s], 16)
            second = pl.multiple_of(small_ref[device, 3 + 4 * s], 16)
            a = rows_ref[pl.ds(first, 16), :]
            b = rows_ref[pl.ds(second, 16), :]
            chunk = jnp.concatenate([a[:8], jnp.where(low, a[8:], b[8:]), b[:8]], 0)
            o_ref[s * NB + device] = chunk.astype(BF16)


def whiten(received, table, ones, taper):
    return pl.pallas_call(
        whiten_kernel,
        out_shape=jax.ShapeDtypeStruct((2 * NB, CHUNK, LANES), BF16),
        in_specs=[pl.BlockSpec(memory_space=pltpu.VMEM)] * 4,
        out_specs=pl.BlockSpec(memory_space=pltpu.VMEM),
        scratch_shapes=[
            pltpu.VMEM((8 * NB, LANES), F32),
            pltpu.VMEM((NB, LANES), jnp.int32),
            pltpu.SMEM((NB, LANES), jnp.int32),
            pltpu.VMEM((2 * F // LANES, 2 * LANES, LANES), F32),
            pltpu.VMEM((16 * NB, LANES), F32),
            pltpu.SemaphoreType.DMA,
        ],
        compiler_params=pltpu.CompilerParams(vmem_limit_bytes=24 * 2**20),
        cost_estimate=pl.CostEstimate(flops=600_000_000, bytes_accessed=4_000_000, transcendentals=100_000),
        name="whiten",
    )(received, table, ones, taper)


GROUP = 8
PIECES = 4
JOBS = (2, 4, 4, 4)


def lags_kernel(pairs_ref, g_ref, back_ref, o_ref, flat_ref, a_ref, b_ref, cross0_ref, cross1_ref):
    step = pl.program_id(0)
    last = pl.num_programs(0) - 1

    def spread(value):
        return jnp.broadcast_to(value, (16, LANES)).astype(BF16)

    def total(terms):
        return ((terms[0] + terms[1]) + (terms[2] + terms[3])) + (terms[4] + terms[5])

    def cross(channel, k, tile, cross_ref):
        ar, ai = [], []
        for win in range(NWIN):
            at = (win // WIN_DEV) * CB + channel
            row = (win % WIN_DEV) * 4 + tile
            ar.append(spread(a_ref[at, row : row + 1, :]))
            ai.append(spread(a_ref[at, row + 2 : row + 3, :]))
        for start in range(0, CB, 16):
            real, imag = [], []
            for win in range(NWIN):
                br = b_ref[win * 4 + tile, start : start + 16]
                bi = b_ref[win * 4 + tile + 2, start : start + 16]
                real.append(ar[win] * br + ai[win] * bi)
                imag.append(ai[win] * br - ar[win] * bi)
            rows = slice(k * CB + start, k * CB + start + 16)
            cross_ref[rows, tile * LANES : (tile + 1) * LANES] = total(real)
            cross_ref[rows, F + tile * LANES : F + (tile + 1) * LANES] = total(imag)

    def both(ready_ref, next_ref):
        jobs = [] if next_ref is None else [(k, tile) for k in range(GROUP) for tile in range(F // LANES)]

        def run(chosen):
            for k, tile in chosen:
                cross(step * GROUP + k, k, tile, next_ref)

        if ready_ref is None:
            run(jobs)
            return
        width = LAGS // PIECES
        done = 0
        for piece in range(PIECES):
            run(jobs[done : done + JOBS[piece]])
            done += JOBS[piece]
            cols = slice(piece * width, (piece + 1) * width)
            lags = jnp.dot(ready_ref[...], back_ref[:, cols], preferred_element_type=F32)
            o_ref[:, :, cols] = lags.astype(BF16).reshape(GROUP, CB, width)
        run(jobs[done:])

    @pl.when(step == 0)
    def _():
        mine = lax.axis_index("tm")
        first = pairs_ref[mine, 0, 0] & (NB - 2)
        second = pairs_ref[mine, 0, 1] & (NB - 2)

        @pl.loop(0, CB, unroll=4)
        def _(source):
            for group in range(2):
                value = g_ref[group * CB + source].astype(F32)
                a_ref[group * CB + (source ^ first)] = value
                start = (group * CB + (source ^ second)) * CHUNK
                flat_ref[pl.ds(pl.multiple_of(start, 8), CHUNK), :] = value

        for group in range(2):
            for row in range(12):
                start = group * CB * CHUNK + (16 + row if row < 8 else 4 + row)
                b_ref[group * 12 + row] = flat_ref[pl.ds(start, CB, stride=CHUNK), :].astype(BF16)
        both(None, cross0_ref)

    @pl.when((step > 0) & (step < last) & (step % 2 == 1))
    def _():
        both(cross0_ref, cross1_ref)

    @pl.when((step > 0) & (step < last) & (step % 2 == 0))
    def _():
        both(cross1_ref, cross0_ref)

    @pl.when(step == last)
    def _():
        both(cross1_ref, None)


def pair_lags(block_pairs, gathered, back):
    return pl.pallas_call(
        lags_kernel,
        grid=(CB // GROUP + 1,),
        out_shape=jax.ShapeDtypeStruct((CB, CB, LAGS), BF16),
        in_specs=[
            pl.BlockSpec(memory_space=pltpu.SMEM),
            pl.BlockSpec(memory_space=pltpu.VMEM),
            pl.BlockSpec(memory_space=pltpu.VMEM),
        ],
        out_specs=pl.BlockSpec((GROUP, CB, LAGS), lambda g: (jnp.maximum(g - 1, 0), 0, 0)),
        scratch_shapes=[
            pltpu.VMEM((2 * CB * CHUNK, LANES), F32),
            pltpu.VMEM((2 * CB, CHUNK, LANES), F32),
            pltpu.VMEM((NWIN * 4, CB, LANES), BF16),
            pltpu.VMEM((GROUP * CB, 2 * F), BF16),
            pltpu.VMEM((GROUP * CB, 2 * F), BF16),
        ],
        compiler_params=pltpu.CompilerParams(vmem_limit_bytes=32 * 2**20),
        cost_estimate=pl.CostEstimate(flops=4_400_000_000, bytes_accessed=12_000_000, transcendentals=0),
        name="pair_lags",
    )(block_pairs, gathered, back)


def solution(mesh):
    basis_np = time_basis()
    table_np = block_tables(basis_np).astype(jnp.bfloat16)
    back_np = lag_table().astype(jnp.bfloat16)

    def per_device(strain, live_mask, block_pairs):
        basis = jnp.asarray(basis_np.T.astype(np.float32))
        ones = jnp.asarray(smoothing_ones().astype(jnp.bfloat16))
        taper = jnp.asarray(np.tile(band_weights(), 2)[None, :].astype(np.float32))
        coefs = project(strain, live_mask, block_pairs, basis)
        with jax.named_scope("channels_exchange"):
            received = lax.all_to_all(coefs, "chan", 0, 0, tiled=True)
        chosen = whiten(received, jnp.asarray(table_np), ones, taper)
        with jax.named_scope("pairs_exchange"):
            gathered = lax.all_to_all(chosen, ("tm", "chan"), 0, 0, tiled=True)
        return pair_lags(block_pairs, gathered, jnp.asarray(back_np)).reshape(1, 1, CB, CB, LAGS)

    in_specs = (P("tm", "chan", None), P("chan"), P(None, "chan", None))
    out_specs = P("tm", "chan", None, None, None)
    return jax.shard_map(per_device, mesh=mesh, in_specs=in_specs, out_specs=out_specs, check_vma=False)
```

```python
import functools
import math

import jax
import jax.numpy as jnp
import numpy as np
from jax import lax
from jax.experimental import pallas as pl
from jax.experimental.pallas import tpu as pltpu
from jax.sharding import PartitionSpec as P

CB = 64
W = 16000
NB = 64
WIN_DEV = 3
NWIN = 6
K0 = 64
F = 256
HALF = 32
WIDTH = F + 2 * HALF
LAGS = 1024
SAMPLES = W // NB
RANK = 24
LAG_RANK = 64
UNITS = 5
ROWS = 8 * UNITS
CHUNK = 24
LANES = 128
TILES = CB * NB // LANES
EPS = 1e-05
F32 = jnp.float32
BF16 = jnp.bfloat16


def prolate(size, band, count):
    places = np.arange(size)
    main = ((size - 1 - 2 * places) / 2.0) ** 2 * np.cos(2 * np.pi * band / W)
    side = places[1:] * (size - places[1:]) / 2.0
    _, vectors = np.linalg.eigh(np.diag(main) + np.diag(side, 1) + np.diag(side, -1))
    basis = vectors[:, ::-1][:, :count]
    mid = size // 2
    centre = np.where(np.arange(count) % 2 == 0, basis[mid] + basis[mid - 1], basis[mid] - basis[mid - 1])
    return basis * np.sign(centre)[None, :]


def time_basis():
    return prolate(SAMPLES, K0 - HALF + WIDTH, RANK)


def lag_basis():
    return prolate(LAGS, K0 + F, LAG_RANK)


def block_tables(basis):
    local = np.arange(SAMPLES)
    bins = np.arange(K0 - HALF, K0 - HALF + WIDTH)
    out = np.empty((2 * WIDTH, RANK // 8, NB, 8))
    for block in range(NB):
        index = ((block * SAMPLES + local)[:, None] * bins[None, :]) % W
        angles = 2 * np.pi / W * index
        table = np.concatenate([np.cos(angles), -np.sin(angles)], 1)
        out[:, :, block, :] = (table.T @ basis).reshape(2 * WIDTH, RANK // 8, 8)
    return out.reshape(2 * WIDTH, RANK * NB)


def lag_table():
    freqs = (K0 + np.arange(F))[:, None]
    steps = (np.arange(LAGS) - LAGS // 2)[None, :]
    angles = 2 * np.pi / W * (freqs * steps % W)
    factor = 1.0 / math.sqrt(WIN_DEV * F)
    return np.concatenate([np.cos(angles) * factor, -np.sin(angles) * factor], 0)


def smoothing_ones():
    rows = np.arange(F)[:, None]
    cols = np.arange(WIDTH)[None, :]
    return (np.abs(cols - rows - HALF) <= HALF).astype(np.float32)


def band_weights():
    freqs = np.arange(F) + 0.5
    ramp = np.minimum(freqs, F - freqs) / (F / 4.0)
    return np.where(ramp < 1.0, 0.5 - 0.5 * np.cos(np.pi * ramp), 1.0)


def project_kernel(parts, pairs_hbm, live_hbm, basis_ref, x_hbm, o_ref, x_ref, z_ref, pairs_ref, live_ref, sems):
    per = TILES // parts
    width = CB * NB // parts
    copies = []
    for c in range(parts):
        cols = pl.ds(c * width, width)
        copies.append(pltpu.make_async_copy(x_hbm.at[:, :, cols], x_ref.at[:, :, cols], sems.at[c]))
    small = [
        pltpu.make_async_copy(pairs_hbm, pairs_ref, sems.at[parts]),
        pltpu.make_async_copy(live_hbm, live_ref, sems.at[parts + 1]),
    ]
    for copy in copies + small:
        copy.start()
    block = lax.axis_index("chan")
    place = lax.broadcasted_iota(jnp.int32, (1, SAMPLES), 1) + block * SAMPLES
    hann = 0.5 - 0.5 * jnp.cos((2.0 * math.pi / W) * place.astype(F32))
    table = (basis_ref[...] * hann).astype(BF16)
    lane = lax.broadcasted_iota(jnp.int32, (16, LANES), 1)
    masks = [((lane >> bit) & 1) == 1 for bit in range(6)]

    def exchange(groups, bits, base):
        for bit in bits:
            stride = 1 << (bit - base)
            for v in range(len(groups[0])):
                if v & stride:
                    continue
                for z in groups:
                    x0, x1 = z[v], z[v | stride]
                    if bit:
                        z[v] = jnp.where(masks[bit], x1, x0)
                        z[v | stride] = jnp.where(masks[bit], x0, x1)
                    else:
                        z[v] = jnp.where(masks[0], pltpu.roll(x1, 1, 1), x0)
                        z[v | stride] = jnp.where(masks[0], x1, pltpu.roll(x0, LANES - 1, 1))

    count = 2 * per
    local = count.bit_length() - 1
    zero = jnp.zeros((8, LANES), BF16)
    for c in range(parts):
        copies[c].wait()
        coef = [
            jnp.dot(table, x_ref[win, :, c * width : (c + 1) * width], preferred_element_type=F32).astype(BF16)
            for win in range(WIN_DEV)
        ]
        groups = [[], [], []]
        for tile in range(per):
            part = [coef[win][:, tile * LANES : (tile + 1) * LANES] for win in range(WIN_DEV)]
            for h in range(2):
                groups[0].append(part[h][:16])
                groups[1].append(jnp.concatenate([part[h][16:], part[2][8 * h : 8 * h + 8]], 0))
                groups[2].append(jnp.concatenate([part[2][16:] if h == 0 else zero, zero], 0))
        exchange(groups, range(local), 0)
        for k in range(3):
            for v in range(count):
                z_ref[k, c * count + v] = groups[k][v]
    for copy in small:
        copy.wait()
    lane = lax.broadcasted_iota(jnp.int32, (8, LANES), 1)
    even = block & (NB - 2)
    extra = jnp.zeros((8, LANES), F32)
    for s in range(2):
        for side in range(2):
            value = pairs_ref[s, 0, side].astype(F32)
            extra = jnp.where(lane == 1 + 4 * s + 2 * side, value, extra)
    for first in range(0, count, 4):
        groups = [[z_ref[k, v + count * c] for c in range(parts)] for k in range(3) for v in range(first, first + 4)]
        exchange(groups, range(local, 6), local)
        for k in range(3):
            for v in range(4):
                for c in range(parts):
                    slab = first + v + count * c
                    value = groups[k * 4 + v][c]
                    if k < 2:
                        o_ref[slab, 16 * k : 16 * k + 16] = value
                    else:
                        added = jnp.where(lane == 9, live_ref[slab ^ even].astype(F32), extra)
                        o_ref[slab, 32:40] = (value[:8].astype(F32) + added).astype(BF16)


def project(strain, live_mask, block_pairs, basis):
    parts = 4
    return pl.pallas_call(
        functools.partial(project_kernel, parts),
        out_shape=jax.ShapeDtypeStruct((CB, ROWS, LANES), BF16),
        in_specs=[
            pl.BlockSpec(memory_space=pltpu.HBM),
            pl.BlockSpec(memory_space=pltpu.HBM),
            pl.BlockSpec(memory_space=pltpu.VMEM),
            pl.BlockSpec(memory_space=pltpu.HBM),
        ],
        out_specs=pl.BlockSpec(memory_space=pltpu.VMEM),
        scratch_shapes=[
            pltpu.VMEM((WIN_DEV, SAMPLES, CB * NB), BF16),
            pltpu.VMEM((3, CB, 16, LANES), BF16),
            pltpu.SMEM((2, 1, 2), jnp.int32),
            pltpu.SMEM((CB,), jnp.int32),
            pltpu.SemaphoreType.DMA((parts + 2,)),
        ],
        compiler_params=pltpu.CompilerParams(vmem_limit_bytes=58 * 2**20),
        cost_estimate=pl.CostEstimate(flops=400_000_000, bytes_accessed=7_000_000, transcendentals=0),
        name="project",
    )(block_pairs, live_mask, basis, strain)


def slot(index, device):
    return ((index & 1) << 5) | ((index ^ device) >> 1)


def whiten_kernel(r_ref, table_ref, ones_ref, taper_ref, o_ref, extra_ref, index_ref, small_ref, spec_ref, rows_ref, sem):
    me = lax.axis_index("chan")
    received = r_ref[...].astype(F32)
    unit = [received[:, 8 * u : 8 * u + 8].reshape(8 * NB, LANES) for u in range(UNITS)]
    extra_ref[...] = unit[4]
    extra = extra_ref[pl.ds(0, NB, stride=8), :]
    index_ref[...] = slot(extra.astype(jnp.int32) & (NB - 1), me) * 16
    copy = pltpu.make_async_copy(index_ref, small_ref, sem)
    copy.start()
    place = lax.broadcasted_iota(jnp.int32, (NB, NB), 0)
    wanted = slot(lax.broadcasted_iota(jnp.int32, (NB, NB), 1), me)
    order = jnp.where(place == wanted, 1.0, 0.0).astype(BF16)
    live = jnp.dot(order, extra.astype(BF16), preferred_element_type=F32)[:, 9:10]
    left = jnp.concatenate(unit[:3], 0)
    right = jnp.concatenate([unit[3], pltpu.roll(unit[3], LANES - 1, 1), unit[4]], 0)
    operand = jnp.concatenate([left, right], 1).astype(BF16)
    raw = jnp.dot(table_ref[...], operand, preferred_element_type=F32)
    real, imag = raw[:WIDTH], raw[WIDTH:]
    magnitude = jnp.sqrt(real * real + imag * imag)
    ones = ones_ref[...]
    total = jnp.zeros((F, 2 * LANES), F32)
    rest = magnitude
    for _ in range(2):
        piece = rest.astype(BF16)
        rest = rest - piece.astype(F32)
        total = total + jnp.dot(ones, piece, preferred_element_type=F32)
    weight = 1.0 / (total * (1.0 / (2 * HALF + 1)) + EPS)
    for tile in range(2 * F // LANES):
        part = real if tile < F // LANES else imag
        start = tile * LANES % F
        picked = part[HALF + start : HALF + start + LANES] * weight[start : start + LANES]
        spec_ref[tile] = picked.T
    for win, start in enumerate((0, 1, LANES)):
        for tile in range(2 * F // LANES):
            cols = slice(tile * LANES, (tile + 1) * LANES)
            value = spec_ref[tile, pl.ds(start, NB, stride=2), :] * taper_ref[:, cols] * live
            rows_ref[pl.ds(win * 4 + tile, NB, stride=16), :] = value
            if win == 2:
                rows_ref[pl.ds(12 + tile, NB, stride=16), :] = value
    copy.wait()
    low = lax.broadcasted_iota(jnp.int32, (8, LANES), 0) < 4

    @pl.loop(0, NB, unroll=8)
    def _(device):
        for s in range(2):
            first = pl.multiple_of(small_ref[device, 1 + 4 * s], 16)
            second = pl.multiple_of(small_ref[device, 3 + 4 * s], 16)
            a = rows_ref[pl.ds(first, 16), :]
            b = rows_ref[pl.ds(second, 16), :]
            chunk = jnp.concatenate([a[:8], jnp.where(low, a[8:], b[8:]), b[:8]], 0)
            o_ref[s * NB + device] = chunk.astype(BF16)


def whiten(received, table, ones, taper):
    return pl.pallas_call(
        whiten_kernel,
        out_shape=jax.ShapeDtypeStruct((2 * NB, CHUNK, LANES), BF16),
        in_specs=[pl.BlockSpec(memory_space=pltpu.VMEM)] * 4,
        out_specs=pl.BlockSpec(memory_space=pltpu.VMEM),
        scratch_shapes=[
            pltpu.VMEM((8 * NB, LANES), F32),
            pltpu.VMEM((NB, LANES), jnp.int32),
            pltpu.SMEM((NB, LANES), jnp.int32),
            pltpu.VMEM((2 * F // LANES, 2 * LANES, LANES), F32),
            pltpu.VMEM((16 * NB, LANES), F32),
            pltpu.SemaphoreType.DMA,
        ],
        compiler_params=pltpu.CompilerParams(vmem_limit_bytes=24 * 2**20),
        cost_estimate=pl.CostEstimate(flops=600_000_000, bytes_accessed=4_000_000, transcendentals=100_000),
        name="whiten",
    )(received, table, ones, taper)


GROUP = 8
PIECES = 4
JOBS = (2, 4, 4, 4)


def lags_kernel(pairs_ref, g_ref, reduce_ref, back_ref, o_ref, flat_ref, a_ref, b_ref, cross0_ref, cross1_ref, low0_ref, low1_ref):
    step = pl.program_id(0)
    last = pl.num_programs(0) - 1

    def spread(value):
        return jnp.broadcast_to(value, (16, LANES)).astype(BF16)

    def total(terms):
        return ((terms[0] + terms[1]) + (terms[2] + terms[3])) + (terms[4] + terms[5])

    def cross(channel, k, tile, cross_ref):
        ar, ai = [], []
        for win in range(NWIN):
            at = (win // WIN_DEV) * CB + channel
            row = (win % WIN_DEV) * 4 + tile
            ar.append(spread(a_ref[at, row : row + 1, :]))
            ai.append(spread(a_ref[at, row + 2 : row + 3, :]))
        for start in range(0, CB, 16):
            real, imag = [], []
            for win in range(NWIN):
                br = b_ref[win * 4 + tile, start : start + 16]
                bi = b_ref[win * 4 + tile + 2, start : start + 16]
                real.append(ar[win] * br + ai[win] * bi)
                imag.append(ai[win] * br - ar[win] * bi)
            rows = slice(k * CB + start, k * CB + start + 16)
            cross_ref[rows, tile * LANES : (tile + 1) * LANES] = total(real)
            cross_ref[rows, F + tile * LANES : F + (tile + 1) * LANES] = total(imag)

    def stage(next_ref, ready_ref, low_ref, done_ref):
        jobs = [] if next_ref is None else [(k, tile) for k in range(GROUP) for tile in range(F // LANES)]

        def run(chosen):
            for k, tile in chosen:
                cross(step * GROUP + k, k, tile, next_ref)

        if ready_ref is not None:
            low_ref[...] = jnp.dot(ready_ref[...], reduce_ref[...], preferred_element_type=F32).astype(BF16)
        width = LAGS // PIECES
        done = 0
        for piece in range(PIECES if done_ref is not None else 0):
            run(jobs[done : done + JOBS[piece]])
            done += JOBS[piece]
            cols = slice(piece * width, (piece + 1) * width)
            lags = jnp.dot(done_ref[...], back_ref[:, cols], preferred_element_type=F32)
            o_ref[:, :, cols] = lags.astype(BF16).reshape(GROUP, CB, width)
        run(jobs[done:])

    @pl.when(step == 0)
    def _():
        mine = lax.axis_index("tm")
        first = pairs_ref[mine, 0, 0] & (NB - 2)
        second = pairs_ref[mine, 0, 1] & (NB - 2)

        @pl.loop(0, CB, unroll=4)
        def _(source):
            for group in range(2):
                value = g_ref[group * CB + source].astype(F32)
                a_ref[group * CB + (source ^ first)] = value
                start = (group * CB + (source ^ second)) * CHUNK
                flat_ref[pl.ds(pl.multiple_of(start, 8), CHUNK), :] = value

        for group in range(2):
            for row in range(12):
                start = group * CB * CHUNK + (16 + row if row < 8 else 4 + row)
                b_ref[group * 12 + row] = flat_ref[pl.ds(start, CB, stride=CHUNK), :].astype(BF16)
        stage(cross0_ref, None, None, None)

    @pl.when(step == 1)
    def _():
        stage(cross1_ref, cross0_ref, low0_ref, None)

    @pl.when((step > 1) & (step < last - 1) & (step % 2 == 0))
    def _():
        stage(cross0_ref, cross1_ref, low1_ref, low0_ref)

    @pl.when((step > 1) & (step < last - 1) & (step % 2 == 1))
    def _():
        stage(cross1_ref, cross0_ref, low0_ref, low1_ref)

    @pl.when(step == last - 1)
    def _():
        stage(None, cross1_ref, low1_ref, low0_ref)

    @pl.when(step == last)
    def _():
        stage(None, None, None, low1_ref)


def pair_lags(block_pairs, gathered, reduce, back):
    return pl.pallas_call(
        lags_kernel,
        grid=(CB // GROUP + 2,),
        out_shape=jax.ShapeDtypeStruct((CB, CB, LAGS), BF16),
        in_specs=[
            pl.BlockSpec(memory_space=pltpu.SMEM),
            pl.BlockSpec(memory_space=pltpu.VMEM),
            pl.BlockSpec(memory_space=pltpu.VMEM),
            pl.BlockSpec(memory_space=pltpu.VMEM),
        ],
        out_specs=pl.BlockSpec((GROUP, CB, LAGS), lambda g: (jnp.maximum(g - 2, 0), 0, 0)),
        scratch_shapes=[
            pltpu.VMEM((2 * CB * CHUNK, LANES), F32),
            pltpu.VMEM((2 * CB, CHUNK, LANES), F32),
            pltpu.VMEM((NWIN * 4, CB, LANES), BF16),
            pltpu.VMEM((GROUP * CB, 2 * F), BF16),
            pltpu.VMEM((GROUP * CB, 2 * F), BF16),
            pltpu.VMEM((GROUP * CB, LAG_RANK), BF16),
            pltpu.VMEM((GROUP * CB, LAG_RANK), BF16),
        ],
        compiler_params=pltpu.CompilerParams(vmem_limit_bytes=32 * 2**20),
        cost_estimate=pl.CostEstimate(flops=900_000_000, bytes_accessed=12_000_000, transcendentals=0),
        name="pair_lags",
    )(block_pairs, gathered, reduce, back)


def solution(mesh):
    basis_np = time_basis()
    table_np = block_tables(basis_np).astype(jnp.bfloat16)
    lag_np = lag_basis()
    reduce_np = (lag_table() @ lag_np).astype(jnp.bfloat16)
    back_np = lag_np.T.astype(jnp.bfloat16)

    def per_device(strain, live_mask, block_pairs):
        basis = jnp.asarray(basis_np.T.astype(np.float32))
        ones = jnp.asarray(smoothing_ones().astype(jnp.bfloat16))
        taper = jnp.asarray(np.tile(band_weights(), 2)[None, :].astype(np.float32))
        coefs = project(strain, live_mask, block_pairs, basis)
        with jax.named_scope("channels_exchange"):
            received = lax.all_to_all(coefs, "chan", 0, 0, tiled=True)
        chosen = whiten(received, jnp.asarray(table_np), ones, taper)
        with jax.named_scope("pairs_exchange"):
            gathered = lax.all_to_all(chosen, ("tm", "chan"), 0, 0, tiled=True)
        return pair_lags(block_pairs, gathered, jnp.asarray(reduce_np), jnp.asarray(back_np)).reshape(1, 1, CB, CB, LAGS)

    in_specs = (P("tm", "chan", None), P("chan"), P(None, "chan", None))
    out_specs = P("tm", "chan", None, None, None)
    return jax.shard_map(per_device, mesh=mesh, in_specs=in_specs, out_specs=out_specs, check_vma=False)
```

```python
import functools
import math

import jax
import jax.numpy as jnp
import numpy as np
from jax import lax
from jax.experimental import pallas as pl
from jax.experimental.pallas import tpu as pltpu
from jax.sharding import PartitionSpec as P

CB = 64
W = 16000
NB = 64
WIN_DEV = 3
NWIN = 6
K0 = 64
F = 256
HALF = 32
WIDTH = F + 2 * HALF
LAGS = 1024
SAMPLES = W // NB
RANK = 24
LAG_RANK = 64
UNITS = 5
ROWS = 8 * UNITS
CHUNK = 24
LANES = 128
TILES = CB * NB // LANES
EPS = 1e-05
F32 = jnp.float32
BF16 = jnp.bfloat16


def prolate(size, band, count):
    places = np.arange(size)
    main = ((size - 1 - 2 * places) / 2.0) ** 2 * np.cos(2 * np.pi * band / W)
    side = places[1:] * (size - places[1:]) / 2.0
    _, vectors = np.linalg.eigh(np.diag(main) + np.diag(side, 1) + np.diag(side, -1))
    basis = vectors[:, ::-1][:, :count]
    mid = size // 2
    centre = np.where(np.arange(count) % 2 == 0, basis[mid] + basis[mid - 1], basis[mid] - basis[mid - 1])
    return basis * np.sign(centre)[None, :]


def time_basis():
    return prolate(SAMPLES, K0 - HALF + WIDTH, RANK)


def lag_basis():
    return prolate(LAGS, K0 + F, LAG_RANK)


def block_tables(basis):
    local = np.arange(SAMPLES)
    bins = np.arange(K0 - HALF, K0 - HALF + WIDTH)
    out = np.empty((2 * WIDTH, RANK // 8, NB, 8))
    for block in range(NB):
        index = ((block * SAMPLES + local)[:, None] * bins[None, :]) % W
        angles = 2 * np.pi / W * index
        table = np.concatenate([np.cos(angles), -np.sin(angles)], 1)
        out[:, :, block, :] = (table.T @ basis).reshape(2 * WIDTH, RANK // 8, 8)
    return out.reshape(2 * WIDTH, RANK * NB)


def lag_table():
    freqs = (K0 + np.arange(F))[:, None]
    steps = (np.arange(LAGS) - LAGS // 2)[None, :]
    angles = 2 * np.pi / W * (freqs * steps % W)
    factor = 1.0 / math.sqrt(WIN_DEV * F)
    return np.concatenate([np.cos(angles) * factor, -np.sin(angles) * factor], 0)


def smoothing_ones():
    rows = np.arange(F)[:, None]
    cols = np.arange(WIDTH)[None, :]
    return (np.abs(cols - rows - HALF) <= HALF).astype(np.float32)


def band_weights():
    freqs = np.arange(F) + 0.5
    ramp = np.minimum(freqs, F - freqs) / (F / 4.0)
    return np.where(ramp < 1.0, 0.5 - 0.5 * np.cos(np.pi * ramp), 1.0)


def project_kernel(parts, pairs_hbm, live_hbm, basis_ref, x_hbm, o_ref, x_ref, z_ref, pairs_ref, live_ref, sems):
    per = TILES // parts
    width = CB * NB // parts
    copies = []
    for c in range(parts):
        cols = pl.ds(c * width, width)
        copies.append(pltpu.make_async_copy(x_hbm.at[:, :, cols], x_ref.at[:, :, cols], sems.at[c]))
    small = [
        pltpu.make_async_copy(pairs_hbm, pairs_ref, sems.at[parts]),
        pltpu.make_async_copy(live_hbm, live_ref, sems.at[parts + 1]),
    ]
    for copy in copies + small:
        copy.start()
    block = lax.axis_index("chan")
    place = lax.broadcasted_iota(jnp.int32, (1, SAMPLES), 1) + block * SAMPLES
    hann = 0.5 - 0.5 * jnp.cos((2.0 * math.pi / W) * place.astype(F32))
    table = (basis_ref[...] * hann).astype(BF16)
    lane = lax.broadcasted_iota(jnp.int32, (16, LANES), 1)
    masks = [((lane >> bit) & 1) == 1 for bit in range(6)]

    def exchange(groups, bits, base):
        for bit in bits:
            stride = 1 << (bit - base)
            for v in range(len(groups[0])):
                if v & stride:
                    continue
                for z in groups:
                    x0, x1 = z[v], z[v | stride]
                    if bit:
                        z[v] = jnp.where(masks[bit], x1, x0)
                        z[v | stride] = jnp.where(masks[bit], x0, x1)
                    else:
                        z[v] = jnp.where(masks[0], pltpu.roll(x1, 1, 1), x0)
                        z[v | stride] = jnp.where(masks[0], x1, pltpu.roll(x0, LANES - 1, 1))

    count = 2 * per
    local = count.bit_length() - 1
    zero = jnp.zeros((8, LANES), BF16)
    for c in range(parts):
        copies[c].wait()
        coef = [
            jnp.dot(table, x_ref[win, :, c * width : (c + 1) * width], preferred_element_type=F32).astype(BF16)
            for win in range(WIN_DEV)
        ]
        groups = [[], [], []]
        for tile in range(per):
            part = [coef[win][:, tile * LANES : (tile + 1) * LANES] for win in range(WIN_DEV)]
            for h in range(2):
                groups[0].append(part[h][:16])
                groups[1].append(jnp.concatenate([part[h][16:], part[2][8 * h : 8 * h + 8]], 0))
                groups[2].append(jnp.concatenate([part[2][16:] if h == 0 else zero, zero], 0))
        exchange(groups, range(local), 0)
        for k in range(3):
            for v in range(count):
                z_ref[k, c * count + v] = groups[k][v]
    for copy in small:
        copy.wait()
    lane = lax.broadcasted_iota(jnp.int32, (8, LANES), 1)
    even = block & (NB - 2)
    extra = jnp.zeros((8, LANES), F32)
    for s in range(2):
        for side in range(2):
            value = pairs_ref[s, 0, side].astype(F32)
            extra = jnp.where(lane == 1 + 4 * s + 2 * side, value, extra)
    for first in range(0, count, 4):
        groups = [[z_ref[k, v + count * c] for c in range(parts)] for k in range(3) for v in range(first, first + 4)]
        exchange(groups, range(local, 6), local)
        for k in range(3):
            for v in range(4):
                for c in range(parts):
                    slab = first + v + count * c
                    value = groups[k * 4 + v][c]
                    if k < 2:
                        o_ref[slab, 16 * k : 16 * k + 16] = value
                    else:
                        added = jnp.where(lane == 9, live_ref[slab ^ even].astype(F32), extra)
                        o_ref[slab, 32:40] = (value[:8].astype(F32) + added).astype(BF16)


def project(strain, live_mask, block_pairs, basis):
    parts = 4
    return pl.pallas_call(
        functools.partial(project_kernel, parts),
        out_shape=jax.ShapeDtypeStruct((CB, ROWS, LANES), BF16),
        in_specs=[
            pl.BlockSpec(memory_space=pltpu.HBM),
            pl.BlockSpec(memory_space=pltpu.HBM),
            pl.BlockSpec(memory_space=pltpu.VMEM),
            pl.BlockSpec(memory_space=pltpu.HBM),
        ],
        out_specs=pl.BlockSpec(memory_space=pltpu.VMEM),
        scratch_shapes=[
            pltpu.VMEM((WIN_DEV, SAMPLES, CB * NB), BF16),
            pltpu.VMEM((3, CB, 16, LANES), BF16),
            pltpu.SMEM((2, 1, 2), jnp.int32),
            pltpu.SMEM((CB,), jnp.int32),
            pltpu.SemaphoreType.DMA((parts + 2,)),
        ],
        compiler_params=pltpu.CompilerParams(vmem_limit_bytes=58 * 2**20),
        cost_estimate=pl.CostEstimate(flops=400_000_000, bytes_accessed=7_000_000, transcendentals=0),
        name="project",
    )(block_pairs, live_mask, basis, strain)


def slot(index, device):
    return ((index & 1) << 5) | ((index ^ device) >> 1)


def whiten_kernel(r_ref, table_ref, ones_ref, taper_ref, o_ref, extra_ref, index_ref, small_ref, spec_ref, rows_ref, sem):
    me = lax.axis_index("chan")
    received = r_ref[...].astype(F32)
    unit = [received[:, 8 * u : 8 * u + 8].reshape(8 * NB, LANES) for u in range(UNITS)]
    extra_ref[...] = unit[4]
    extra = extra_ref[pl.ds(0, NB, stride=8), :]
    index_ref[...] = slot(extra.astype(jnp.int32) & (NB - 1), me) * 16
    copy = pltpu.make_async_copy(index_ref, small_ref, sem)
    copy.start()
    place = lax.broadcasted_iota(jnp.int32, (NB, NB), 0)
    wanted = slot(lax.broadcasted_iota(jnp.int32, (NB, NB), 1), me)
    order = jnp.where(place == wanted, 1.0, 0.0).astype(BF16)
    live = jnp.dot(order, extra.astype(BF16), preferred_element_type=F32)[:, 9:10]
    left = jnp.concatenate(unit[:3], 0)
    right = jnp.concatenate([unit[3], pltpu.roll(unit[3], LANES - 1, 1), unit[4]], 0)
    operand = jnp.concatenate([left, right], 1).astype(BF16)
    raw = jnp.dot(table_ref[...], operand, preferred_element_type=F32)
    real, imag = raw[:WIDTH], raw[WIDTH:]
    magnitude = jnp.sqrt(real * real + imag * imag)
    ones = ones_ref[...]
    total = jnp.zeros((F, 2 * LANES), F32)
    rest = magnitude
    for _ in range(2):
        piece = rest.astype(BF16)
        rest = rest - piece.astype(F32)
        total = total + jnp.dot(ones, piece, preferred_element_type=F32)
    weight = 1.0 / (total * (1.0 / (2 * HALF + 1)) + EPS)
    for tile in range(2 * F // LANES):
        part = real if tile < F // LANES else imag
        start = tile * LANES % F
        picked = part[HALF + start : HALF + start + LANES] * weight[start : start + LANES]
        spec_ref[tile] = picked.T
    for win, start in enumerate((0, 1, LANES)):
        for tile in range(2 * F // LANES):
            cols = slice(tile * LANES, (tile + 1) * LANES)
            value = spec_ref[tile, pl.ds(start, NB, stride=2), :] * taper_ref[:, cols] * live
            rows_ref[pl.ds(win * 4 + tile, NB, stride=16), :] = value
            if win == 2:
                rows_ref[pl.ds(12 + tile, NB, stride=16), :] = value
    copy.wait()
    low = lax.broadcasted_iota(jnp.int32, (8, LANES), 0) < 4

    @pl.loop(0, NB, unroll=8)
    def _(device):
        for s in range(2):
            first = pl.multiple_of(small_ref[device, 1 + 4 * s], 16)
            second = pl.multiple_of(small_ref[device, 3 + 4 * s], 16)
            a = rows_ref[pl.ds(first, 16), :]
            b = rows_ref[pl.ds(second, 16), :]
            chunk = jnp.concatenate([a[:8], jnp.where(low, a[8:], b[8:]), b[:8]], 0)
            o_ref[s * NB + device] = chunk.astype(BF16)


def whiten(received, table, ones, taper):
    return pl.pallas_call(
        whiten_kernel,
        out_shape=jax.ShapeDtypeStruct((2 * NB, CHUNK, LANES), BF16),
        in_specs=[pl.BlockSpec(memory_space=pltpu.VMEM)] * 4,
        out_specs=pl.BlockSpec(memory_space=pltpu.VMEM),
        scratch_shapes=[
            pltpu.VMEM((8 * NB, LANES), F32),
            pltpu.VMEM((NB, LANES), jnp.int32),
            pltpu.SMEM((NB, LANES), jnp.int32),
            pltpu.VMEM((2 * F // LANES, 2 * LANES, LANES), F32),
            pltpu.VMEM((16 * NB, LANES), F32),
            pltpu.SemaphoreType.DMA,
        ],
        compiler_params=pltpu.CompilerParams(vmem_limit_bytes=24 * 2**20),
        cost_estimate=pl.CostEstimate(flops=600_000_000, bytes_accessed=4_000_000, transcendentals=100_000),
        name="whiten",
    )(received, table, ones, taper)


GROUP = 8
PIECES = 4
JOBS = (2, 4, 4, 4)


def lags_kernel(pairs_ref, g_ref, reduce_ref, back_ref, o_ref, flat_ref, a_ref, b_ref, cross0_ref, cross1_ref, low0_ref, low1_ref):
    step = pl.program_id(0)
    last = pl.num_programs(0) - 1

    def spread(value):
        return jnp.broadcast_to(value, (16, LANES)).astype(BF16)

    def total(terms):
        return ((terms[0] + terms[1]) + (terms[2] + terms[3])) + (terms[4] + terms[5])

    def cross(channel, k, tile, cross_ref):
        ar, ai = [], []
        for win in range(NWIN):
            at = (win // WIN_DEV) * CB + channel
            row = (win % WIN_DEV) * 4 + tile
            ar.append(spread(a_ref[at, row : row + 1, :]))
            ai.append(spread(a_ref[at, row + 2 : row + 3, :]))
        for start in range(0, CB, 16):
            real, imag = [], []
            for win in range(NWIN):
                br = b_ref[win * 4 + tile, start : start + 16]
                bi = b_ref[win * 4 + tile + 2, start : start + 16]
                real.append(ar[win] * br + ai[win] * bi)
                imag.append(ai[win] * br - ar[win] * bi)
            rows = slice(k * CB + start, k * CB + start + 16)
            cross_ref[rows, tile * LANES : (tile + 1) * LANES] = total(real)
            cross_ref[rows, F + tile * LANES : F + (tile + 1) * LANES] = total(imag)

    def stage(next_ref, ready_ref, low_ref, done_ref):
        jobs = [] if next_ref is None else [(k, tile) for k in range(GROUP) for tile in range(F // LANES)]

        def run(chosen):
            for k, tile in chosen:
                cross(step * GROUP + k, k, tile, next_ref)

        if ready_ref is not None:
            low_ref[...] = jnp.dot(ready_ref[...], reduce_ref[...], preferred_element_type=F32).astype(BF16)
        width = LAGS // PIECES
        done = 0
        for piece in range(PIECES if done_ref is not None else 0):
            run(jobs[done : done + JOBS[piece]])
            done += JOBS[piece]
            cols = slice(piece * width, (piece + 1) * width)
            lags = jnp.dot(done_ref[...], back_ref[:, cols], preferred_element_type=F32)
            o_ref[:, :, cols] = lags.astype(BF16).reshape(GROUP, CB, width)
        run(jobs[done:])

    @pl.when(step == 0)
    def _():
        mine = lax.axis_index("tm")
        pair = jnp.where(mine == 0, pairs_ref[0], pairs_ref[1]).astype(F32)
        side = lax.broadcasted_iota(jnp.int32, pair.shape, 1)
        first = jnp.sum(jnp.where(side == 0, pair, 0.0)).astype(jnp.int32) & (NB - 2)
        second = jnp.sum(jnp.where(side == 1, pair, 0.0)).astype(jnp.int32) & (NB - 2)

        @pl.loop(0, CB, unroll=4)
        def _(source):
            for group in range(2):
                value = g_ref[group * CB + source].astype(F32)
                a_ref[group * CB + (source ^ first)] = value
                start = (group * CB + (source ^ second)) * CHUNK
                flat_ref[pl.ds(pl.multiple_of(start, 8), CHUNK), :] = value

        for group in range(2):
            for row in range(12):
                start = group * CB * CHUNK + (16 + row if row < 8 else 4 + row)
                b_ref[group * 12 + row] = flat_ref[pl.ds(start, CB, stride=CHUNK), :].astype(BF16)
        stage(cross0_ref, None, None, None)

    @pl.when(step == 1)
    def _():
        stage(cross1_ref, cross0_ref, low0_ref, None)

    @pl.when((step > 1) & (step < last - 1) & (step % 2 == 0))
    def _():
        stage(cross0_ref, cross1_ref, low1_ref, low0_ref)

    @pl.when((step > 1) & (step < last - 1) & (step % 2 == 1))
    def _():
        stage(cross1_ref, cross0_ref, low0_ref, low1_ref)

    @pl.when(step == last - 1)
    def _():
        stage(None, cross1_ref, low1_ref, low0_ref)

    @pl.when(step == last)
    def _():
        stage(None, None, None, low1_ref)


def pair_lags(block_pairs, gathered, reduce, back):
    return pl.pallas_call(
        lags_kernel,
        grid=(CB // GROUP + 2,),
        out_shape=jax.ShapeDtypeStruct((CB, CB, LAGS), BF16),
        in_specs=[
            pl.BlockSpec(memory_space=pltpu.VMEM),
            pl.BlockSpec(memory_space=pltpu.VMEM),
            pl.BlockSpec(memory_space=pltpu.VMEM),
            pl.BlockSpec(memory_space=pltpu.VMEM),
        ],
        out_specs=pl.BlockSpec((GROUP, CB, LAGS), lambda g: (jnp.maximum(g - 2, 0), 0, 0)),
        scratch_shapes=[
            pltpu.VMEM((2 * CB * CHUNK, LANES), F32),
            pltpu.VMEM((2 * CB, CHUNK, LANES), F32),
            pltpu.VMEM((NWIN * 4, CB, LANES), BF16),
            pltpu.VMEM((GROUP * CB, 2 * F), BF16),
            pltpu.VMEM((GROUP * CB, 2 * F), BF16),
            pltpu.VMEM((GROUP * CB, LAG_RANK), BF16),
            pltpu.VMEM((GROUP * CB, LAG_RANK), BF16),
        ],
        compiler_params=pltpu.CompilerParams(vmem_limit_bytes=32 * 2**20),
        cost_estimate=pl.CostEstimate(flops=900_000_000, bytes_accessed=12_000_000, transcendentals=0),
        name="pair_lags",
    )(block_pairs, gathered, reduce, back)


def solution(mesh):
    basis_np = time_basis()
    table_np = block_tables(basis_np).astype(jnp.bfloat16)
    lag_np = lag_basis()
    reduce_np = (lag_table() @ lag_np).astype(jnp.bfloat16)
    back_np = lag_np.T.astype(jnp.bfloat16)

    def per_device(strain, live_mask, block_pairs):
        basis = jnp.asarray(basis_np.T.astype(np.float32))
        ones = jnp.asarray(smoothing_ones().astype(jnp.bfloat16))
        taper = jnp.asarray(np.tile(band_weights(), 2)[None, :].astype(np.float32))
        coefs = project(strain, live_mask, block_pairs, basis)
        with jax.named_scope("channels_exchange"):
            received = lax.all_to_all(coefs, "chan", 0, 0, tiled=True)
        chosen = whiten(received, jnp.asarray(table_np), ones, taper)
        with jax.named_scope("pairs_exchange"):
            gathered = lax.all_to_all(chosen, ("tm", "chan"), 0, 0, tiled=True)
        return pair_lags(block_pairs, gathered, jnp.asarray(reduce_np), jnp.asarray(back_np)).reshape(1, 1, CB, CB, LAGS)

    in_specs = (P("tm", "chan", None), P("chan"), P(None, "chan", None))
    out_specs = P("tm", "chan", None, None, None)
    return jax.shard_map(per_device, mesh=mesh, in_specs=in_specs, out_specs=out_specs, check_vma=False)
```

```python
import functools
import math

import jax
import jax.numpy as jnp
import numpy as np
from jax import lax
from jax.experimental import pallas as pl
from jax.experimental.pallas import tpu as pltpu
from jax.sharding import PartitionSpec as P

CB = 64
W = 16000
NB = 64
WIN_DEV = 3
NWIN = 6
K0 = 64
F = 256
HALF = 32
WIDTH = F + 2 * HALF
LAGS = 1024
SAMPLES = W // NB
RANK = 24
LAG_RANK = 64
UNITS = 5
ROWS = 8 * UNITS
CHUNK = 24
LANES = 128
TILES = CB * NB // LANES
EPS = 1e-05
F32 = jnp.float32
BF16 = jnp.bfloat16


def prolate(size, band, count):
    places = np.arange(size)
    main = ((size - 1 - 2 * places) / 2.0) ** 2 * np.cos(2 * np.pi * band / W)
    side = places[1:] * (size - places[1:]) / 2.0
    _, vectors = np.linalg.eigh(np.diag(main) + np.diag(side, 1) + np.diag(side, -1))
    basis = vectors[:, ::-1][:, :count]
    mid = size // 2
    centre = np.where(np.arange(count) % 2 == 0, basis[mid] + basis[mid - 1], basis[mid] - basis[mid - 1])
    return basis * np.sign(centre)[None, :]


def time_basis():
    return prolate(SAMPLES, K0 - HALF + WIDTH, RANK)


def lag_basis():
    return prolate(LAGS, K0 + F, LAG_RANK)


def block_tables(basis):
    local = np.arange(SAMPLES)
    bins = np.arange(K0 - HALF, K0 - HALF + WIDTH)
    out = np.empty((2 * WIDTH, RANK // 8, NB, 8))
    for block in range(NB):
        index = ((block * SAMPLES + local)[:, None] * bins[None, :]) % W
        angles = 2 * np.pi / W * index
        table = np.concatenate([np.cos(angles), -np.sin(angles)], 1)
        out[:, :, block, :] = (table.T @ basis).reshape(2 * WIDTH, RANK // 8, 8)
    return out.reshape(2 * WIDTH, RANK * NB)


def lag_table():
    freqs = (K0 + np.arange(F))[:, None]
    steps = (np.arange(LAGS) - LAGS // 2)[None, :]
    angles = 2 * np.pi / W * (freqs * steps % W)
    factor = 1.0 / math.sqrt(WIN_DEV * F)
    return np.concatenate([np.cos(angles) * factor, -np.sin(angles) * factor], 0)


def smoothing_ones():
    rows = np.arange(F)[:, None]
    cols = np.arange(WIDTH)[None, :]
    return (np.abs(cols - rows - HALF) <= HALF).astype(np.float32)


def band_weights():
    freqs = np.arange(F) + 0.5
    ramp = np.minimum(freqs, F - freqs) / (F / 4.0)
    return np.where(ramp < 1.0, 0.5 - 0.5 * np.cos(np.pi * ramp), 1.0)


def project_kernel(parts, pairs_hbm, live_hbm, basis_ref, x_hbm, o_ref, x_ref, z_ref, pairs_ref, live_ref, sems):
    per = TILES // parts
    width = CB * NB // parts
    copies = []
    for c in range(parts):
        cols = pl.ds(c * width, width)
        copies.append(pltpu.make_async_copy(x_hbm.at[:, :, cols], x_ref.at[:, :, cols], sems.at[c]))
    small = [
        pltpu.make_async_copy(pairs_hbm, pairs_ref, sems.at[parts]),
        pltpu.make_async_copy(live_hbm, live_ref, sems.at[parts + 1]),
    ]
    for copy in copies + small:
        copy.start()
    block = lax.axis_index("chan")
    place = lax.broadcasted_iota(jnp.int32, (1, SAMPLES), 1) + block * SAMPLES
    hann = 0.5 - 0.5 * jnp.cos((2.0 * math.pi / W) * place.astype(F32))
    table = (basis_ref[...] * hann).astype(BF16)
    lane = lax.broadcasted_iota(jnp.int32, (16, LANES), 1)
    masks = [((lane >> bit) & 1) == 1 for bit in range(6)]

    def exchange(groups, bits, base):
        for bit in bits:
            stride = 1 << (bit - base)
            for v in range(len(groups[0])):
                if v & stride:
                    continue
                for z in groups:
                    x0, x1 = z[v], z[v | stride]
                    if bit:
                        z[v] = jnp.where(masks[bit], x1, x0)
                        z[v | stride] = jnp.where(masks[bit], x0, x1)
                    else:
                        z[v] = jnp.where(masks[0], pltpu.roll(x1, 1, 1), x0)
                        z[v | stride] = jnp.where(masks[0], x1, pltpu.roll(x0, LANES - 1, 1))

    count = 2 * per
    local = count.bit_length() - 1
    zero = jnp.zeros((8, LANES), BF16)
    for c in range(parts):
        copies[c].wait()
        coef = [
            jnp.dot(table, x_ref[win, :, c * width : (c + 1) * width], preferred_element_type=F32).astype(BF16)
            for win in range(WIN_DEV)
        ]
        groups = [[], [], []]
        for tile in range(per):
            part = [coef[win][:, tile * LANES : (tile + 1) * LANES] for win in range(WIN_DEV)]
            for h in range(2):
                groups[0].append(part[h][:16])
                groups[1].append(jnp.concatenate([part[h][16:], part[2][8 * h : 8 * h + 8]], 0))
                groups[2].append(jnp.concatenate([part[2][16:] if h == 0 else zero, zero], 0))
        exchange(groups, range(local), 0)
        for k in range(3):
            for v in range(count):
                z_ref[k, c * count + v] = groups[k][v]
    for copy in small:
        copy.wait()
    lane = lax.broadcasted_iota(jnp.int32, (8, LANES), 1)
    even = block & (NB - 2)
    extra = jnp.zeros((8, LANES), F32)
    for s in range(2):
        for side in range(2):
            value = pairs_ref[s, 0, side].astype(F32)
            extra = jnp.where(lane == 1 + 4 * s + 2 * side, value, extra)
    for first in range(0, count, 4):
        groups = [[z_ref[k, v + count * c] for c in range(parts)] for k in range(3) for v in range(first, first + 4)]
        exchange(groups, range(local, 6), local)
        for k in range(3):
            for v in range(4):
                for c in range(parts):
                    slab = first + v + count * c
                    value = groups[k * 4 + v][c]
                    if k < 2:
                        o_ref[slab, 16 * k : 16 * k + 16] = value
                    else:
                        added = jnp.where(lane == 9, live_ref[slab ^ even].astype(F32), extra)
                        o_ref[slab, 32:40] = (value[:8].astype(F32) + added).astype(BF16)


def project(strain, live_mask, block_pairs, basis):
    parts = 4
    return pl.pallas_call(
        functools.partial(project_kernel, parts),
        out_shape=jax.ShapeDtypeStruct((CB, ROWS, LANES), BF16),
        in_specs=[
            pl.BlockSpec(memory_space=pltpu.HBM),
            pl.BlockSpec(memory_space=pltpu.HBM),
            pl.BlockSpec(memory_space=pltpu.VMEM),
            pl.BlockSpec(memory_space=pltpu.HBM),
        ],
        out_specs=pl.BlockSpec(memory_space=pltpu.VMEM),
        scratch_shapes=[
            pltpu.VMEM((WIN_DEV, SAMPLES, CB * NB), BF16),
            pltpu.VMEM((3, CB, 16, LANES), BF16),
            pltpu.SMEM((2, 1, 2), jnp.int32),
            pltpu.SMEM((CB,), jnp.int32),
            pltpu.SemaphoreType.DMA((parts + 2,)),
        ],
        compiler_params=pltpu.CompilerParams(vmem_limit_bytes=58 * 2**20),
        cost_estimate=pl.CostEstimate(flops=400_000_000, bytes_accessed=7_000_000, transcendentals=0),
        name="project",
    )(block_pairs, live_mask, basis, strain)


def slot(index, device):
    return ((index & 1) << 5) | ((index ^ device) >> 1)


def whiten_kernel(r_ref, table_ref, ones_ref, taper_ref, o_ref, extra_ref, index_ref, small_ref, spec_ref, rows_ref, sem):
    me = lax.axis_index("chan")
    received = r_ref[...].astype(F32)
    unit = [received[:, 8 * u : 8 * u + 8].reshape(8 * NB, LANES) for u in range(UNITS)]
    extra_ref[...] = unit[4]
    extra = extra_ref[pl.ds(0, NB, stride=8), :]
    index_ref[...] = slot(extra.astype(jnp.int32) & (NB - 1), me) * 16
    copy = pltpu.make_async_copy(index_ref, small_ref, sem)
    copy.start()
    place = lax.broadcasted_iota(jnp.int32, (NB, NB), 0)
    wanted = slot(lax.broadcasted_iota(jnp.int32, (NB, NB), 1), me)
    order = jnp.where(place == wanted, 1.0, 0.0).astype(BF16)
    live = jnp.dot(order, extra.astype(BF16), preferred_element_type=F32)[:, 9:10]
    left = jnp.concatenate(unit[:3], 0)
    right = jnp.concatenate([unit[3], pltpu.roll(unit[3], LANES - 1, 1), unit[4]], 0)
    operand = jnp.concatenate([left, right], 1).astype(BF16)
    raw = jnp.dot(table_ref[...], operand, preferred_element_type=F32)
    real, imag = raw[:WIDTH], raw[WIDTH:]
    magnitude = jnp.sqrt(real * real + imag * imag)
    ones = ones_ref[...]
    total = jnp.zeros((F, 2 * LANES), F32)
    rest = magnitude
    for _ in range(2):
        piece = rest.astype(BF16)
        rest = rest - piece.astype(F32)
        total = total + jnp.dot(ones, piece, preferred_element_type=F32)
    weight = 1.0 / (total * (1.0 / (2 * HALF + 1)) + EPS)
    for tile in range(2 * F // LANES):
        part = real if tile < F // LANES else imag
        start = tile * LANES % F
        picked = part[HALF + start : HALF + start + LANES] * weight[start : start + LANES]
        spec_ref[tile] = picked.T
    for win, start in enumerate((0, 1, LANES)):
        for tile in range(2 * F // LANES):
            cols = slice(tile * LANES, (tile + 1) * LANES)
            value = spec_ref[tile, pl.ds(start, NB, stride=2), :] * taper_ref[:, cols] * live
            rows_ref[pl.ds(win * 4 + tile, NB, stride=16), :] = value
            if win == 2:
                rows_ref[pl.ds(12 + tile, NB, stride=16), :] = value
    copy.wait()
    low = lax.broadcasted_iota(jnp.int32, (8, LANES), 0) < 4

    @pl.loop(0, NB, unroll=8)
    def _(device):
        for s in range(2):
            first = pl.multiple_of(small_ref[device, 1 + 4 * s], 16)
            second = pl.multiple_of(small_ref[device, 3 + 4 * s], 16)
            a = rows_ref[pl.ds(first, 16), :]
            b = rows_ref[pl.ds(second, 16), :]
            chunk = jnp.concatenate([a[:8], jnp.where(low, a[8:], b[8:]), b[:8]], 0)
            o_ref[s * NB + device] = chunk.astype(BF16)


def whiten(received, table, ones, taper):
    return pl.pallas_call(
        whiten_kernel,
        out_shape=jax.ShapeDtypeStruct((2 * NB, CHUNK, LANES), BF16),
        in_specs=[pl.BlockSpec(memory_space=pltpu.VMEM)] * 4,
        out_specs=pl.BlockSpec(memory_space=pltpu.VMEM),
        scratch_shapes=[
            pltpu.VMEM((8 * NB, LANES), F32),
            pltpu.VMEM((NB, LANES), jnp.int32),
            pltpu.SMEM((NB, LANES), jnp.int32),
            pltpu.VMEM((2 * F // LANES, 2 * LANES, LANES), F32),
            pltpu.VMEM((16 * NB, LANES), F32),
            pltpu.SemaphoreType.DMA,
        ],
        compiler_params=pltpu.CompilerParams(vmem_limit_bytes=24 * 2**20),
        cost_estimate=pl.CostEstimate(flops=600_000_000, bytes_accessed=4_000_000, transcendentals=100_000),
        name="whiten",
    )(received, table, ones, taper)


GROUP = 8
PIECES = 4
JOBS = (2, 4, 4, 4)


def lags_kernel(pairs_ref, g_ref, reduce_ref, back_ref, o_ref, flat_ref, b_ref, cross0_ref, cross1_ref, low0_ref, low1_ref, turn_ref):
    step = pl.program_id(0)
    last = pl.num_programs(0) - 1

    def spread(value):
        return jnp.broadcast_to(value, (16, LANES)).astype(BF16)

    def total(terms):
        return ((terms[0] + terms[1]) + (terms[2] + terms[3])) + (terms[4] + terms[5])

    def cross(channel, k, tile, cross_ref):
        ar, ai = [], []
        for win in range(NWIN):
            at = ((win // WIN_DEV) * CB + (channel ^ turn_ref[0])) * CHUNK
            row = (win % WIN_DEV) * 4 + tile
            for rows, place in ((ar, row), (ai, row + 2)):
                start = pl.multiple_of(at + place // 8 * 8, 8)
                rows.append(spread(flat_ref[pl.ds(start, 8), :][place % 8 : place % 8 + 1]))
        for start in range(0, CB, 16):
            real, imag = [], []
            for win in range(NWIN):
                br = b_ref[win * 4 + tile, start : start + 16]
                bi = b_ref[win * 4 + tile + 2, start : start + 16]
                real.append(ar[win] * br + ai[win] * bi)
                imag.append(ai[win] * br - ar[win] * bi)
            rows = slice(k * CB + start, k * CB + start + 16)
            cross_ref[rows, tile * LANES : (tile + 1) * LANES] = total(real)
            cross_ref[rows, F + tile * LANES : F + (tile + 1) * LANES] = total(imag)

    def stage(next_ref, ready_ref, low_ref, done_ref):
        jobs = [] if next_ref is None else [(k, tile) for k in range(GROUP) for tile in range(F // LANES)]

        def run(chosen):
            for k, tile in chosen:
                cross(step * GROUP + k, k, tile, next_ref)

        if ready_ref is not None:
            low_ref[...] = jnp.dot(ready_ref[...], reduce_ref[...], preferred_element_type=F32).astype(BF16)
        width = LAGS // PIECES
        done = 0
        for piece in range(PIECES if done_ref is not None else 0):
            run(jobs[done : done + JOBS[piece]])
            done += JOBS[piece]
            cols = slice(piece * width, (piece + 1) * width)
            lags = jnp.dot(done_ref[...], back_ref[:, cols], preferred_element_type=F32)
            o_ref[:, :, cols] = lags.astype(BF16).reshape(GROUP, CB, width)
        run(jobs[done:])

    @pl.when(step == 0)
    def _():
        mine = lax.axis_index("tm")
        pair = jnp.where(mine == 0, pairs_ref[0], pairs_ref[1]).astype(F32)
        side = lax.broadcasted_iota(jnp.int32, pair.shape, 1)
        first = jnp.sum(jnp.where(side == 0, pair, 0.0)).astype(jnp.int32) & (NB - 2)
        second = jnp.sum(jnp.where(side == 1, pair, 0.0)).astype(jnp.int32) & (NB - 2)
        turn_ref[0] = first ^ second

        @pl.loop(0, CB, unroll=4)
        def _(source):
            for group in range(2):
                value = g_ref[group * CB + source].astype(F32)
                start = (group * CB + (source ^ second)) * CHUNK
                flat_ref[pl.ds(pl.multiple_of(start, 8), CHUNK), :] = value

        for group in range(2):
            for row in range(12):
                start = group * CB * CHUNK + (16 + row if row < 8 else 4 + row)
                b_ref[group * 12 + row] = flat_ref[pl.ds(start, CB, stride=CHUNK), :].astype(BF16)
        stage(cross0_ref, None, None, None)

    @pl.when(step == 1)
    def _():
        stage(cross1_ref, cross0_ref, low0_ref, None)

    @pl.when((step > 1) & (step < last - 1) & (step % 2 == 0))
    def _():
        stage(cross0_ref, cross1_ref, low1_ref, low0_ref)

    @pl.when((step > 1) & (step < last - 1) & (step % 2 == 1))
    def _():
        stage(cross1_ref, cross0_ref, low0_ref, low1_ref)

    @pl.when(step == last - 1)
    def _():
        stage(None, cross1_ref, low1_ref, low0_ref)

    @pl.when(step == last)
    def _():
        stage(None, None, None, low1_ref)


def pair_lags(block_pairs, gathered, reduce, back):
    return pl.pallas_call(
        lags_kernel,
        grid=(CB // GROUP + 2,),
        out_shape=jax.ShapeDtypeStruct((CB, CB, LAGS), BF16),
        in_specs=[
            pl.BlockSpec(memory_space=pltpu.VMEM),
            pl.BlockSpec(memory_space=pltpu.VMEM),
            pl.BlockSpec(memory_space=pltpu.VMEM),
            pl.BlockSpec(memory_space=pltpu.VMEM),
        ],
        out_specs=pl.BlockSpec((GROUP, CB, LAGS), lambda g: (jnp.maximum(g - 2, 0), 0, 0)),
        scratch_shapes=[
            pltpu.VMEM((2 * CB * CHUNK, LANES), F32),
            pltpu.VMEM((NWIN * 4, CB, LANES), BF16),
            pltpu.VMEM((GROUP * CB, 2 * F), BF16),
            pltpu.VMEM((GROUP * CB, 2 * F), BF16),
            pltpu.VMEM((GROUP * CB, LAG_RANK), BF16),
            pltpu.VMEM((GROUP * CB, LAG_RANK), BF16),
            pltpu.SMEM((1,), jnp.int32),
        ],
        compiler_params=pltpu.CompilerParams(vmem_limit_bytes=32 * 2**20),
        cost_estimate=pl.CostEstimate(flops=900_000_000, bytes_accessed=12_000_000, transcendentals=0),
        name="pair_lags",
    )(block_pairs, gathered, reduce, back)


def solution(mesh):
    basis_np = time_basis()
    table_np = block_tables(basis_np).astype(jnp.bfloat16)
    lag_np = lag_basis()
    reduce_np = (lag_table() @ lag_np).astype(jnp.bfloat16)
    back_np = lag_np.T.astype(jnp.bfloat16)

    def per_device(strain, live_mask, block_pairs):
        basis = jnp.asarray(basis_np.T.astype(np.float32))
        ones = jnp.asarray(smoothing_ones().astype(jnp.bfloat16))
        taper = jnp.asarray(np.tile(band_weights(), 2)[None, :].astype(np.float32))
        coefs = project(strain, live_mask, block_pairs, basis)
        with jax.named_scope("channels_exchange"):
            received = lax.all_to_all(coefs, "chan", 0, 0, tiled=True)
        chosen = whiten(received, jnp.asarray(table_np), ones, taper)
        with jax.named_scope("pairs_exchange"):
            gathered = lax.all_to_all(chosen, ("tm", "chan"), 0, 0, tiled=True)
        return pair_lags(block_pairs, gathered, jnp.asarray(reduce_np), jnp.asarray(back_np)).reshape(1, 1, CB, CB, LAGS)

    in_specs = (P("tm", "chan", None), P("chan"), P(None, "chan", None))
    out_specs = P("tm", "chan", None, None, None)
    return jax.shard_map(per_device, mesh=mesh, in_specs=in_specs, out_specs=out_specs, check_vma=False)
```
